256 devices in a mesh: elem: 32 (over y, z), mode: 8 (over x, core).
Axes of the slice: x: 4, y: 4, z: 8, core: 2. Of those that a mesh axis runs over, the one named last changes fastest.
Arguments:
- vel_x: float32 [81, 512, 1024], P(None, 'elem', 'mode'), may hold values from -6 to 6
- vel_y: float32 [81, 512, 1024], P(None, 'elem', 'mode'), may hold values from -6 to 6
- metrics: float32 [8, 81, 512], P(None, None, 'elem'), may hold values from -2 to 5, as said below
- slot_order: int32 [512], P('elem'), may hold values from 0 to 15, as said below
Outputs:
- new_vel_x: float32 [81, 512, 1024], P(None, 'elem', 'mode')
- new_vel_y: float32 [81, 512, 1024], P(None, 'elem', 'mode')
The draws below stay inside these ranges and needn't reach their ends.
Inputs may be any that keep to these rules, and one draw needn't show every extreme that they name: `metrics`: rows 0 and 3 lie in 0.5 to 2 and rows 1 and 2 in -0.5 to 0.5; rows 4, 6 and 7 are positive, and |row 5| is at most 0.4 sqrt(row 4 row 6). `slot_order`: each aligned block of 16 entries, one sector's, is a permutation of 0 to 15.
All inputs are finite; a program needn't handle non-finite values.
Results may differ from the reference program's by a relative error of at most 0.0003.
Values sent between devices are 32-bit elements; how exact they have to be, the bound alone decides.
A program may use at most 128 MiB of HBM per device.

```python
import math
import jax
import jax.numpy as jnp
import numpy as np
from jax import lax

ORDER = 8
NP = 9
NODES = 81
RAD = 4
AZ_DEV = 4
MODES = 1024
PLANES = 1536
ITERS = 2
E_DEV = 16
ELEMS = 512
AZI = 128


def log_uniform(key, shape, lower, upper):
    return jnp.exp(jax.random.uniform(key, shape, jnp.float32, math.log(lower), math.log(upper)))


def draw_metrics(key, part):
    key = jax.random.fold_in(key, 11)
    keys = jax.random.split(key, 8)
    shape = (NODES, ELEMS)
    lower = 0.5
    upper = 2.0
    first_x = log_uniform(keys[0], shape, 0.5, 2.0)
    second_x = jax.random.uniform(keys[1], shape, jnp.float32, -0.5, 0.5)
    first_y = jax.random.uniform(keys[2], shape, jnp.float32, -0.5, 0.5)
    second_y = log_uniform(keys[3], shape, 0.5, 2.0)
    stiff_a = log_uniform(keys[4], shape, lower, upper)
    stiff_b = log_uniform(keys[5], shape, lower, upper)
    coupling = jax.random.uniform(keys[6], shape, jnp.float32, -0.4, 0.4) * jnp.sqrt(stiff_a * stiff_b)
    jacobian = log_uniform(keys[7], shape, 0.5 * lower, 0.5 * upper)
    return jnp.stack([first_x, second_x, first_y, second_y, stiff_a, coupling, stiff_b, jacobian]).astype(jnp.float32)


def draw_slot_order(key, part):
    key = jax.random.fold_in(key, 23)
    blocks = ELEMS // E_DEV
    keys = jax.random.split(key, blocks)
    shuffled = jax.vmap(lambda single: jax.random.permutation(single, E_DEV))(keys)
    return shuffled.reshape(-1).astype(jnp.int32)


def shard_levels(stream_key, dims, cuts, smallest, largest):
    loudness = 1.0
    for axis_at, shards_of in cuts:
        draws = jax.random.uniform(jax.random.fold_in(jax.random.fold_in(stream_key, 6), axis_at), (shards_of,), jnp.float32, smallest / len(cuts), largest / len(cuts))
        loudness = loudness * jnp.repeat(jnp.exp(draws), dims[axis_at] // shards_of).reshape((-1,) + (1,) * (len(dims) - 1 - axis_at))
    return loudness


def bell_draw(stream_key, dims, width, limit, cuts=(), held_as=jnp.bfloat16):
    level = shard_levels(stream_key, dims, cuts, -0.22, 0.18) if cuts else 1.0
    entries = jax.random.normal(stream_key, dims, jnp.float32) * width * level
    return jnp.minimum(jnp.maximum(entries, -limit), limit).astype(held_as)


def setup_inputs(seed: int = 0) -> dict:
    key_of = jax.random.split(jax.random.key(seed), 5)
    return {
        "vel_x": bell_draw(key_of[0], (NODES, ELEMS, MODES), 1.0, 6.0, ((1, 32), (2, 8)), jnp.float32),
        "vel_y": bell_draw(key_of[1], (NODES, ELEMS, MODES), 1.0, 6.0, ((1, 32), (2, 8)), jnp.float32),
        "metrics": draw_metrics(jax.random.fold_in(key_of[4], 71), 0),
        "slot_order": draw_slot_order(jax.random.fold_in(key_of[4], 71), 0),
    }


SIGMA = 2.0
WAVE = 64.0
HIGH = lax.Precision.HIGHEST

def legendre_value(order, point):
    previous = 1.0
    current = point
    for degree in range(2, order + 1):
        previous, current = (current, ((2 * degree - 1) * point * current - (degree - 1) * previous) / degree)
    return (current, previous)

def gll_matrix(order):
    points = []
    for index in range(order + 1):
        point = -math.cos(math.pi * index / order)
        for sweep in range(100):
            high, lower = legendre_value(order, point)
            point = point - (point * high - lower) / ((order + 1) * high)
        points.append(point)
    points[0] = -1.0
    points[order] = 1.0
    values = [legendre_value(order, point)[0] for point in points]
    number = order + 1
    matrix = np.zeros((number, number))
    for row_index in range(number):
        for col_index in range(number):
            if row_index != col_index:
                matrix[row_index, col_index] = values[row_index] / (values[col_index] * (points[row_index] - points[col_index]))
    matrix[0, 0] = -order * (order + 1) / 4.0
    matrix[order, order] = order * (order + 1) / 4.0
    return matrix

def basis_table(modes, planes):
    wave_index = jnp.arange(modes, dtype=jnp.int32)
    frequency = (wave_index + 1) // 2
    plane = jnp.arange(planes, dtype=jnp.int32)
    phase = frequency[:, None] * plane[None, :] % planes
    angle = 2.0 * math.pi / planes * phase.astype(jnp.float32)
    even = (wave_index % 2 == 0)[:, None]
    table = jnp.where(even, jnp.cos(angle), jnp.sin(angle))
    factor = jnp.where(wave_index == 0, math.sqrt(1.0 / planes), math.sqrt(2.0 / planes)).astype(jnp.float32)
    return (table * factor[:, None]).astype(jnp.float32)

def derivatives(field, dmatrix, geometry):
    along_i = jnp.einsum('pi,ijem->pjem', dmatrix, field, precision=HIGH)
    along_j = jnp.einsum('qj,ijem->iqem', dmatrix, field, precision=HIGH)
    grad_x = geometry[0][..., None] * along_i + geometry[1][..., None] * along_j
    grad_y = geometry[2][..., None] * along_i + geometry[3][..., None] * along_j
    return (grad_x, grad_y)

def wall_factors(points, radial):
    across = jnp.arange(points, dtype=jnp.int32)[:, None, None]
    along = jnp.arange(points, dtype=jnp.int32)[None, :, None]
    layer = jnp.arange(radial, dtype=jnp.int32)[None, None, :]
    wall = (layer == 0) & (across == 0) | (layer == radial - 1) & (across == points - 1)
    keep = jnp.where(wall, 0.0, 1.0).astype(jnp.float32)
    sides = jnp.where((along == 0) | (along == points - 1), 2.0, 1.0).astype(jnp.float32)
    inside = (across == 0) & (layer > 0) | (across == points - 1) & (layer < radial - 1)
    shared = jnp.where(inside, 2.0, 1.0).astype(jnp.float32)
    weight = keep / (sides * shared)
    return (keep, weight)

def helmholtz_local(field, geometry, shifts, dmatrix):
    along_i = jnp.einsum('pi,cijram->cpjram', dmatrix, field, precision=HIGH)
    along_j = jnp.einsum('qj,cijram->ciqram', dmatrix, field, precision=HIGH)
    g_aa = geometry[0][None, ..., None]
    g_ab = geometry[1][None, ..., None]
    g_bb = geometry[2][None, ..., None]
    jacob = geometry[3][None, ..., None]
    flux_i = g_aa * along_i + g_ab * along_j
    flux_j = g_ab * along_i + g_bb * along_j
    result = jnp.einsum('pi,cpjram->cijram', dmatrix, flux_i, precision=HIGH)
    result = result + jnp.einsum('qj,ciqram->cijram', dmatrix, flux_j, precision=HIGH)
    return result + shifts * jacob * field

def assemble_whole(field, keep):
    last = field.shape[1] - 1
    right = field[:, :, last]
    left = field[:, :, 0]
    shared = right + jnp.roll(left, -1, axis=3)
    field = field.at[:, :, last].set(shared).at[:, :, 0].set(jnp.roll(shared, 1, axis=3))
    outer = field[:, last, :, :-1]
    inner_side = field[:, 0, :, 1:]
    joined = outer + inner_side
    field = field.at[:, last, :, :-1].set(joined).at[:, 0, :, 1:].set(joined)
    return field * keep[None, :, :, :, None, None]

def inner(first, second, weight):
    return lax.optimization_barrier(jnp.sum(first * second * weight[None, :, :, :, None, None], axis=(1, 2, 3, 4)))

def expand(values):
    return values[:, None, None, None, None, :]

def reference(vel_x, vel_y, metrics, slot_order):
    dmatrix = jnp.asarray(gll_matrix(ORDER), jnp.float32)
    table = basis_table(MODES, PLANES)
    blocks = ELEMS // E_DEV

    def nonlinear(pieces):
        part_x, part_y, geometry = pieces
        shaped_x = part_x.reshape(NP, NP, E_DEV, MODES)
        shaped_y = part_y.reshape(NP, NP, E_DEV, MODES)
        geo = geometry.reshape(8, NP, NP, E_DEV)
        xx_dx, xx_dy = derivatives(shaped_x, dmatrix, geo)
        yy_dx, yy_dy = derivatives(shaped_y, dmatrix, geo)
        stacked = jnp.stack([shaped_x, shaped_y, xx_dx, xx_dy, yy_dx, yy_dy])
        planes = jnp.dot(stacked.reshape(-1, MODES), table, precision=HIGH).reshape(6, NP, NP, E_DEV, PLANES)
        first = planes[0] * planes[2] + planes[1] * planes[3]
        second = planes[0] * planes[4] + planes[1] * planes[5]
        products = jnp.stack([first, second]).reshape(-1, PLANES)
        return jnp.dot(products, table.T, precision=HIGH).reshape(2, NODES, E_DEV, MODES)
    blocked_x = jnp.moveaxis(vel_x.reshape(NODES, blocks, E_DEV, MODES), 1, 0)
    blocked_y = jnp.moveaxis(vel_y.reshape(NODES, blocks, E_DEV, MODES), 1, 0)
    blocked_g = jnp.moveaxis(metrics.reshape(8, NODES, blocks, E_DEV), 2, 0)
    nonlin = lax.map(nonlinear, (blocked_x, blocked_y, blocked_g))
    nonlin = jnp.moveaxis(nonlin, 0, 2).reshape(2, NODES, ELEMS, MODES)
    velocity = jnp.stack([vel_x, vel_y])
    source = metrics[7][None, :, :, None] * (SIGMA * velocity - nonlin)
    position = jnp.arange(ELEMS, dtype=jnp.int32) // E_DEV * E_DEV + slot_order.astype(jnp.int32)
    grid_src = source[:, :, position, :].reshape(2, NP, NP, blocks, RAD, AZ_DEV, MODES)
    grid_src = jnp.transpose(grid_src, (0, 1, 2, 4, 3, 5, 6)).reshape(2, NP, NP, RAD, AZI, MODES)
    geometry = metrics[4:8][:, :, position].reshape(4, NP, NP, blocks, RAD, AZ_DEV)
    geometry = jnp.transpose(geometry, (0, 1, 2, 4, 3, 5)).reshape(4, NP, NP, RAD, AZI)
    keep, weight = wall_factors(NP, RAD)
    frequency = ((jnp.arange(MODES, dtype=jnp.int32) + 1) // 2).astype(jnp.float32)
    shifts = SIGMA + (frequency / WAVE) ** 2

    def operator(field):
        return assemble_whole(helmholtz_local(field, geometry, shifts, dmatrix), keep)
    rhs = assemble_whole(grid_src, keep)
    solution = jnp.zeros_like(rhs)
    residual = rhs
    direction = rhs
    norm_now = inner(residual, residual, weight)
    for step in range(ITERS):
        image = operator(direction)
        alpha = norm_now / inner(direction, image, weight)
        solution = solution + expand(alpha) * direction
        residual = residual - expand(alpha) * image
        if step + 1 < ITERS:
            norm_next = inner(residual, residual, weight)
            direction = residual + expand(norm_next / norm_now) * direction
            norm_now = norm_next
    flat = solution.reshape(2, NP, NP, RAD, blocks, AZ_DEV, MODES)
    flat = jnp.transpose(flat, (0, 1, 2, 4, 3, 5, 6)).reshape(2, NODES, ELEMS, MODES)
    result = jnp.zeros((2, NODES, ELEMS, MODES), jnp.float32).at[:, :, position, :].set(flat)
    return (result[0], result[1])
```

```python
import functools
import math

import jax
import jax.numpy as jnp
import ml_dtypes
import numpy as np
from jax import lax
from jax.experimental import pallas as pl
from jax.experimental.pallas import tpu as pltpu
from jax.sharding import PartitionSpec as P

ORDER = 8
NP = ORDER + 1
NODES = NP * NP
ROWS = 88
KROWS = 96
EDGE = NODES - NP
RAD = 4
AZ = 4
ELEMS = 16
MODES = 1024
PLANES = 1536
LANES = 128
CHUNK = 256
GROUPS = 8
ZRING = 8
SIGMA = 2.0
WAVE = 64.0
MESH = pl.DeviceIdType.MESH
F32 = jnp.float32
BF16 = jnp.bfloat16


def legendre_value(order, point):
    previous = 1.0
    current = point
    for degree in range(2, order + 1):
        previous, current = (
            current,
            ((2 * degree - 1) * point * current - (degree - 1) * previous) / degree,
        )
    return (current, previous)


def gll_matrix(order):
    points = []
    for index in range(order + 1):
        point = -math.cos(math.pi * index / order)
        for sweep in range(100):
            high, lower = legendre_value(order, point)
            point = point - (point * high - lower) / ((order + 1) * high)
        points.append(point)
    points[0] = -1.0
    points[order] = 1.0
    values = [legendre_value(order, point)[0] for point in points]
    number = order + 1
    matrix = np.zeros((number, number))
    for row_index in range(number):
        for col_index in range(number):
            if row_index != col_index:
                matrix[row_index, col_index] = values[row_index] / (
                    values[col_index] * (points[row_index] - points[col_index])
                )
    matrix[0, 0] = -order * (order + 1) / 4.0
    matrix[order, order] = order * (order + 1) / 4.0
    return matrix


def halves(array):
    array = np.asarray(array, np.float32)
    high = array.astype(ml_dtypes.bfloat16)
    low = (array - high.astype(np.float32)).astype(ml_dtypes.bfloat16)
    return high, low


@functools.lru_cache(maxsize=None)
def constants():
    wave = np.arange(MODES)
    freq = (wave + 1) // 2
    phase = freq[:, None] * np.arange(PLANES)[None, :] % PLANES
    angle = 2.0 * np.pi / PLANES * phase
    table = np.where((wave % 2 == 0)[:, None], np.cos(angle), np.sin(angle))
    table = table * np.where(wave == 0, math.sqrt(1.0 / PLANES), math.sqrt(2.0 / PLANES))[:, None]
    high, low = halves(table)
    there = np.stack([high, low]).reshape(2, MODES, PLANES // CHUNK, CHUNK).transpose(0, 2, 1, 3)
    back = np.stack([high.T, low.T]).reshape(2, PLANES, MODES // CHUNK, CHUNK).transpose(0, 2, 1, 3)
    dmat = gll_matrix(ORDER).astype(np.float32)
    eye = np.eye(NP, dtype=np.float32)
    grad = np.zeros((2, ROWS, ROWS), np.float32)
    grad[0, :NODES, :NODES] = np.kron(dmat, eye)
    grad[1, :NODES, :NODES] = np.kron(eye, dmat)
    ghigh, glow = halves(grad.reshape(2 * ROWS, ROWS))
    gmat = np.zeros((4 * ROWS, 2 * KROWS), ml_dtypes.bfloat16)
    gmat[: 2 * ROWS, :ROWS] = ghigh
    gmat[: 2 * ROWS, KROWS : KROWS + ROWS] = ghigh
    gmat[2 * ROWS :, :ROWS] = glow
    dhigh, dlow = halves(grad.transpose(2, 0, 1).reshape(ROWS, 2 * ROWS))
    dmat2 = np.zeros((2 * KROWS, 2 * ROWS), ml_dtypes.bfloat16)
    dmat2[:ROWS] = dhigh
    dmat2[KROWS : KROWS + ROWS] = dlow
    return np.ascontiguousarray(there), np.ascontiguousarray(back), gmat, dmat2


def split(value):
    high = value.astype(BF16)
    return high, (value - high.astype(F32)).astype(BF16)


def split_rows(value):
    high = value.astype(BF16).astype(F32)
    gap = jnp.zeros((KROWS - ROWS, value.shape[1]), F32)
    return jnp.concatenate([high, gap, value - high, gap], axis=0).astype(BF16)


def mm(a, b):
    return jnp.dot(a, b, preferred_element_type=F32)


def fold(value):
    total = jnp.sum(value.reshape(ROWS // 8, 8, value.shape[1]), axis=0)
    out = total[:, :LANES]
    for at in range(1, value.shape[1] // LANES):
        out = out + total[:, at * LANES : (at + 1) * LANES]
    return out


def position(rank, second):
    return ((rank % 2) * 2 + second) * AZ + rank // 2


def kernel(
    size_e,
    velx_hbm,
    vely_hbm,
    met_hbm,
    slots,
    there_hbm,
    back_hbm,
    gmat_hbm,
    dmat_hbm,
    out,
    vel,
    met,
    there,
    back,
    gmat,
    dmat,
    snd,
    rv,
    act,
    wave,
    edge,
    pgeo,
    geo,
    wts,
    ret,
    rv2,
    bf,
    yf,
    hs,
    hr,
    acc,
    part,
    gat_z,
    gat_y,
    in_sem,
    s1,
    r1,
    own,
    s2,
    r2,
    hsem,
    hrem,
    as_z,
    ar_z,
    as_y,
    ar_y,
):
    me_e = lax.axis_index("elem")
    me = lax.axis_index("mode")
    chip, core = me // 2, me % 2
    zed, why = me_e % ZRING, me_e // ZRING
    size_y = size_e // ZRING
    left = (me_e + size_e - 1) % size_e
    right = (me_e + 1) % size_e
    peers = [
        (((chip + dc) % 4) * 2 + (core + cc) % 2)
        for dc, cc in ((2, 0), (2, 1), (1, 0), (3, 0), (1, 1), (3, 1), (0, 1))
    ]
    z_peers = [why * ZRING + (zed + k) % ZRING for k in range(1, ZRING)]
    y_peers = [((why + k) % size_y) * ZRING + zed for k in range(1, size_y)]

    loads = [
        pltpu.make_async_copy(velx_hbm, vel.at[0], in_sem.at[0]),
        pltpu.make_async_copy(vely_hbm, vel.at[1], in_sem.at[1]),
        pltpu.make_async_copy(met_hbm, met, in_sem.at[2]),
        pltpu.make_async_copy(gmat_hbm, gmat, in_sem.at[3]),
        pltpu.make_async_copy(dmat_hbm, dmat, in_sem.at[4]),
        pltpu.make_async_copy(there_hbm, there, in_sem.at[5]),
        pltpu.make_async_copy(back_hbm, back, in_sem.at[6]),
    ]
    for copy in loads:
        copy.start()

    tail = jnp.zeros((2, 8, LANES), F32)
    for p in range(ELEMS):
        snd[p, :, ROWS - 8 :, :] = tail
        rv[p // 2, p % 2, :, ROWS - 8 :, :] = tail
        rv2[p, :, EDGE : EDGE + 8, :] = tail
        rv2[p, :, EDGE + 8 :, :] = tail

    barrier = pltpu.get_barrier_semaphore()
    for peer in peers:
        pl.semaphore_signal(barrier, inc=1, device_id=(me_e, peer), device_id_type=MESH)
    for peer in z_peers + y_peers + [left, right]:
        pl.semaphore_signal(barrier, inc=1, device_id=(peer, me), device_id_type=MESH)

    pl.semaphore_wait(barrier, len(peers) + len(z_peers) + len(y_peers) + 2)

    loads[0].wait()
    loads[1].wait()

    def gather(p):
        slot = slots[p]
        for c in range(2):
            snd[p, c, 0:NODES, :] = vel[c, pl.ds(slot, NODES, stride=ELEMS), :]

    sends = []
    arrivals = [[], []]
    locals_ = []
    for e in range(2):
        for k, peer in enumerate(peers):
            p = position(peer, e)
            gather(p)
            copy = pltpu.make_async_remote_copy(
                src_ref=snd.at[p, :, pl.ds(0, NODES)],
                dst_ref=rv.at[me, e, :, pl.ds(0, NODES)],
                send_sem=s1.at[e, k],
                recv_sem=r1.at[e, me],
                device_id=(me_e, peer),
                device_id_type=MESH,
            )
            copy.start()
            sends.append(copy)
        p = position(me, e)
        gather(p)
        copy = pltpu.make_async_copy(
            snd.at[p, :, pl.ds(0, NODES)], rv.at[me, e, :, pl.ds(0, NODES)], own.at[e]
        )
        copy.start()
        locals_.append(copy)
        for k, peer in enumerate(peers):
            arrivals[e].append(
                pltpu.make_async_remote_copy(
                    src_ref=snd.at[0, :, pl.ds(0, NODES)],
                    dst_ref=rv.at[peer, e, :, pl.ds(0, NODES)],
                    send_sem=s1.at[e, k],
                    recv_sem=r1.at[e, peer],
                    device_id=(me_e, peer),
                    device_id_type=MESH,
                )
            )

    loads[2].wait()
    loads[3].wait()
    loads[4].wait()
    row16 = lax.broadcasted_iota(jnp.int32, (ELEMS, LANES), 0)

    def picker(p):
        return jnp.where(row16 == slots[p], 1.0, 0.0).astype(BF16)

    def spread(factors, pick):
        gap = jnp.zeros((ROWS - NODES, ELEMS), F32)
        full = jnp.concatenate([factors, gap], axis=0)
        high = full.astype(BF16)
        rest = full - high.astype(F32)
        mid = rest.astype(BF16)
        low = (rest - mid.astype(F32)).astype(BF16)
        return mm(high, pick) + mm(mid, pick) + mm(low, pick)

    mine = jnp.concatenate([picker(position(me, 0)), picker(position(me, 1))], axis=1)
    jac = spread(met[7], mine)
    for g in range(4):
        full = spread(met[g], mine) * jac
        pgeo[0, g] = full[:, :LANES]
        pgeo[1, g] = full[:, LANES:]

    def spread_row(r, carry):
        pick = jnp.concatenate([picker(r * AZ + a) for a in range(AZ)], axis=1)
        for g in range(4):
            full = spread(met[4 + g], pick)
            for a in range(AZ):
                geo[g, r * AZ + a] = full[:, a * LANES : (a + 1) * LANES]
        return carry

    lax.fori_loop(0, RAD, spread_row, 0)

    node = lax.broadcasted_iota(jnp.int32, (ROWS, LANES), 0)
    along = node % NP
    sides = jnp.where((along == 0) | (along == NP - 1), 0.5, 1.0).astype(F32)
    sides = jnp.where(node < NODES, sides, 0.0)
    first, last = node < NP, node >= EDGE
    wts[0] = jnp.where(first, 0.0, jnp.where(last, 0.5, 1.0)) * sides
    wts[1] = jnp.where(first | last, 0.5, 1.0) * sides
    wts[2] = wts[1]
    wts[3] = jnp.where(last, 0.0, jnp.where(first, 0.5, 1.0)) * sides

    lane = lax.broadcasted_iota(jnp.int32, (1, LANES), 1) + me * LANES
    freq = ((lane + 1) // 2).astype(F32) / WAVE
    lam = SIGMA + freq * freq

    acc[...] = jnp.zeros_like(acc)

    ret_sends = []
    ret_locals = []
    for e in range(2):
        for copy in arrivals[e]:
            copy.wait_recv()
        locals_[e].wait()
        for src in range(GROUPS):
            both = rv[src, e].reshape(2 * ROWS, LANES)
            high, low = split(both)
            act[0 : 2 * ROWS, src * LANES : (src + 1) * LANES] = high
            act[2 * ROWS :, src * LANES : (src + 1) * LANES] = low
        if e == 0:
            loads[5].wait()

        def planes(z, carry, e=e):
            top = mm(act[...], there[0, z])
            field = top[: 2 * ROWS] + top[2 * ROWS :] + mm(act[0 : 2 * ROWS, :], there[1, z])
            u, v = field[:ROWS], field[ROWS:]
            diff = mm(gmat[...], split_rows(jnp.concatenate([u, v], axis=1)))
            diff = diff[: 2 * ROWS] + diff[2 * ROWS :]
            m = [jnp.concatenate([pgeo[e, g]] * (CHUNK // LANES), axis=1) for g in range(4)]
            by_i = u * m[0] + v * m[2]
            by_j = u * m[1] + v * m[3]
            for c in range(2):
                cols = slice(c * CHUNK, (c + 1) * CHUNK)
                prod = by_i * diff[:ROWS, cols] + by_j * diff[ROWS:, cols]
                if e == 0:
                    edge[c, z] = prod[EDGE:]
                else:
                    lower = prod[:16] + edge[c, z]
                    prod = jnp.concatenate([lower, prod[16:]], axis=0)
                if c == 0:
                    keep = prod
            high, low = split(jnp.concatenate([keep, prod], axis=0))
            at = pl.ds(pl.multiple_of(z * CHUNK, CHUNK), CHUNK)
            wave[0 : 2 * ROWS, at] = high
            wave[2 * ROWS :, at] = low
            return carry

        lax.fori_loop(0, PLANES // CHUNK, planes, 0)
        if e == 0:
            loads[6].wait()

        count = EDGE if e == 0 else NODES
        for step, dc in enumerate((2, 1, 3, 0)):
            n = (chip + dc) % 4
            top = mm(wave[...], back[0, n])
            hat = top[: 2 * ROWS] + top[2 * ROWS :] + mm(wave[0 : 2 * ROWS, :], back[1, n])
            for cc in range(2):
                pass
            for half in range(2):
                ret[e, n * 2 + half] = hat[:, half * LANES : (half + 1) * LANES].reshape(2, ROWS, LANES)
            for cc in range(2):
                peer = n * 2 + (core + cc) % 2
                src = ret.at[e, peer, :, pl.ds(0, count)]
                dst = rv2.at[position(me, e), :, pl.ds(0, count)]
                if dc == 0 and cc == 0:
                    copy = pltpu.make_async_copy(src, dst, own.at[2 + e])
                    ret_locals.append(copy)
                else:
                    copy = pltpu.make_async_remote_copy(
                        src_ref=src,
                        dst_ref=dst,
                        send_sem=s2.at[e, step * 2 + cc],
                        recv_sem=r2.at[e, me],
                        device_id=(me_e, peer),
                        device_id_type=MESH,
                    )
                    ret_sends.append(copy)
                copy.start()

    ret_arrivals = []
    for e in range(2):
        count = EDGE if e == 0 else NODES
        for peer in peers:
            ret_arrivals.append(
                pltpu.make_async_remote_copy(
                    src_ref=ret.at[e, 0, :, pl.ds(0, count)],
                    dst_ref=rv2.at[position(peer, e), :, pl.ds(0, count)],
                    send_sem=s2.at[e, 0],
                    recv_sem=r2.at[e, peer],
                    device_id=(me_e, peer),
                    device_id_type=MESH,
                )
            )
    for copy in ret_arrivals:
        copy.wait_recv()
    for copy in ret_locals:
        copy.wait()

    halo_sends = []

    def assemble_start(field, c, which):
        def column(a, carry):
            for r in range(RAD - 1):
                up, down = r * AZ + a, (r + 1) * AZ + a
                joined = field[c, up, EDGE : EDGE + 8] + field[c, down, 0:8]
                corner = field[c, up, EDGE + 8 : NODES] + field[c, down, 8:NP]
                field[c, up, EDGE : EDGE + 8] = joined
                field[c, down, 0:8] = joined
                field[c, up, EDGE + 8 : NODES] = corner
                field[c, down, 8:NP] = corner
            field[c, a, 0:8] = jnp.zeros((8, LANES), F32)
            field[c, a, 8:NP] = jnp.zeros((1, LANES), F32)
            end = (RAD - 1) * AZ + a
            field[c, end, EDGE : EDGE + 8] = jnp.zeros((8, LANES), F32)
            field[c, end, EDGE + 8 : NODES] = jnp.zeros((1, LANES), F32)
            return carry

        lax.fori_loop(0, AZ, column, 0)
        for r in range(RAD):
            hs[which, c, 0, r, 0:NP] = field[c, r * AZ, pl.ds(0, NP, stride=NP), :]
            hs[which, c, 1, r, 0:NP] = field[c, r * AZ + AZ - 1, pl.ds(NP - 1, NP, stride=NP), :]
        copies = []
        for side, peer in ((0, left), (1, right)):
            copy = pltpu.make_async_remote_copy(
                src_ref=hs.at[which, c, side, :, pl.ds(0, NP)],
                dst_ref=hr.at[which, c, side, :, pl.ds(0, NP)],
                send_sem=hsem.at[which, c, side],
                recv_sem=hrem.at[which, c, side],
                device_id=(peer, me),
                device_id_type=MESH,
            )
            copy.start()
            copies.append(copy)
        halo_sends.extend(copies)

        def joints(r, carry):
            for a in range(AZ - 1):
                p = r * AZ + a
                shared = (
                    field[c, p, pl.ds(NP - 1, NP, stride=NP), :]
                    + field[c, p + 1, pl.ds(0, NP, stride=NP), :]
                )
                field[c, p, pl.ds(NP - 1, NP, stride=NP), :] = shared
                field[c, p + 1, pl.ds(0, NP, stride=NP), :] = shared
            return carry

        lax.fori_loop(0, RAD, joints, 0)
        return copies

    def assemble_finish(field, c, which, copies):
        for copy in copies:
            copy.wait_recv()
        for r in range(RAD):
            p = r * AZ + AZ - 1
            at = pl.ds(NP - 1, NP, stride=NP)
            field[c, p, at, :] = field[c, p, at, :] + hr[which, c, 0, r, 0:NP]
            p = r * AZ
            at = pl.ds(0, NP, stride=NP)
            field[c, p, at, :] = field[c, p, at, :] + hr[which, c, 1, r, 0:NP]

    def pair(ref, c, p0, p1):
        return jnp.concatenate([ref[c, p0], ref[c, p1]], axis=1)

    def fluxes(x, p0, p1):
        diff = mm(gmat[...], split_rows(x))
        diff = diff[: 2 * ROWS] + diff[2 * ROWS :]
        x_i, x_j = diff[:ROWS], diff[ROWS:]
        g = [pair(geo, k, p0, p1) for k in range(4)]
        return x_i, x_j, g[0] * x_i + g[1] * x_j, g[1] * x_i + g[2] * x_j, g[3]

    lam2 = jnp.concatenate([lam, lam], axis=1)

    def weights(r):
        return jnp.concatenate([wts[r], wts[r]], axis=1)

    def apply(c, cols):
        def step(r, carry):
            p0, p1 = r * AZ + cols[0], r * AZ + cols[1]
            x = pair(bf, c, p0, p1)
            x_i, x_j, f_i, f_j, jw = fluxes(x, p0, p1)
            high, low = split(jnp.concatenate([f_i, f_j], axis=0))
            top = mm(dmat[...], high)
            y = top[:ROWS] + top[KROWS : KROWS + ROWS] + mm(dmat[0:KROWS, :], low)[:ROWS]
            y = y + lam2 * jw * x
            yf[c, p0] = y[:, :LANES]
            yf[c, p1] = y[:, LANES:]
            acc[c, 0] = acc[c, 0] + fold(x * x * weights(r))
            acc[c, 1] = acc[c, 1] + fold(x * y)
            return carry

        lax.fori_loop(0, RAD, step, 0)

    def energy(c, cols):
        def step(r, carry):
            p0, p1 = r * AZ + cols[0], r * AZ + cols[1]
            y = pair(yf, c, p0, p1)
            y_i, y_j, f_i, f_j, jw = fluxes(y, p0, p1)
            acc[c, 2] = acc[c, 2] + fold(y * y * weights(r))
            acc[c, 3] = acc[c, 3] + fold(f_i * y_i + f_j * y_j + lam2 * jw * y * y)
            return carry

        lax.fori_loop(0, RAD, step, 0)

    def rhs(c):
        def step(p, carry):
            bf[c, p] = (SIGMA * geo[3, p]) * snd[p, c] - rv2[p, c]
            return carry

        lax.fori_loop(0, ELEMS, step, 0)

    inside, outside = (1, 2), (0, AZ - 1)
    flights = []
    for c in range(2):
        rhs(c)
        flights.append(assemble_start(bf, c, 0))
    for c in range(2):
        apply(c, inside)
    next_flights = []
    for c in range(2):
        assemble_finish(bf, c, 0, flights[c])
        apply(c, outside)
        next_flights.append(assemble_start(yf, c, 1))
    for c in range(2):
        energy(c, inside)
    for c in range(2):
        assemble_finish(yf, c, 1, next_flights[c])
        energy(c, outside)

    sums = jnp.concatenate(
        [jnp.sum(acc[c, k], axis=0, keepdims=True) for c in range(2) for k in range(4)], axis=0
    )

    def exchange(value, slot, group, send_sem, recv_sem, ranks, mine_at, to_device):
        part[slot] = value
        copies = []
        for k, (peer, at) in enumerate(ranks):
            copy = pltpu.make_async_remote_copy(
                src_ref=part.at[slot],
                dst_ref=group.at[mine_at],
                send_sem=send_sem.at[k],
                recv_sem=recv_sem.at[mine_at],
                device_id=(peer, me),
                device_id_type=MESH,
            )
            copy.start()
            copies.append(copy)
        total = value
        for k, (peer, at) in enumerate(ranks):
            pltpu.make_async_remote_copy(
                src_ref=part.at[slot],
                dst_ref=group.at[at],
                send_sem=send_sem.at[k],
                recv_sem=recv_sem.at[at],
                device_id=(peer, me),
                device_id_type=MESH,
            ).wait_recv()
        group[mine_at] = value
        total = group[0]
        for at in range(1, len(ranks) + 1):
            total = total + group[at]
        return total, copies

    z_ranks = [(peer, peer % ZRING) for peer in z_peers]
    y_ranks = [(peer, peer // ZRING) for peer in y_peers]
    sums, more = exchange(sums, 0, gat_z, as_z, ar_z, z_ranks, zed, None)
    halo_sends.extend(more)
    if y_ranks:
        sums, more = exchange(sums, 1, gat_y, as_y, ar_y, y_ranks, why, None)
        halo_sends.extend(more)

    for c in range(2):
        m0, m1, m2, m3 = (sums[c * 4 + k : c * 4 + k + 1] for k in range(4))
        alpha = m0 / m1
        grown = alpha * alpha * m2 - m0
        scale = 1.0 + grown / m0
        below = scale * scale * m1 - 2.0 * scale * alpha * m2 + alpha * alpha * m3
        beyond = grown / below
        on_b = alpha + beyond * scale
        on_y = -beyond * alpha

        def combine(p, carry, c=c, on_b=on_b, on_y=on_y):
            out[c, p] = on_b * bf[c, p] + on_y * yf[c, p]
            return carry

        lax.fori_loop(0, ELEMS, combine, 0)

    for copy in sends + ret_sends + halo_sends:
        copy.wait_send()


def scatter_kernel(slots, grid, out_x, out_y):
    for p in range(ELEMS):
        slot = slots[p]
        out_x[pl.ds(slot, NODES, stride=ELEMS), :] = grid[0, p, 0:NODES]
        out_y[pl.ds(slot, NODES, stride=ELEMS), :] = grid[1, p, 0:NODES]


def body(size_e, vel_x, vel_y, metrics, slot_order):
    there, back, gmat, dmat = constants()
    any_space = pl.BlockSpec(memory_space=pl.ANY)
    vmem = pl.BlockSpec(memory_space=pltpu.VMEM)
    smem = pl.BlockSpec(memory_space=pltpu.SMEM)
    dma = pltpu.SemaphoreType.DMA
    size_y = size_e // ZRING
    rows = NODES * ELEMS
    grid = pl.pallas_call(
        functools.partial(kernel, size_e),
        out_shape=jax.ShapeDtypeStruct((2, ELEMS, ROWS, LANES), F32),
        in_specs=[any_space] * 3 + [smem] + [any_space] * 4,
        out_specs=vmem,
        scratch_shapes=[
            pltpu.VMEM((2, rows, LANES), F32),
            pltpu.VMEM((8, NODES, ELEMS), F32),
            pltpu.VMEM(there.shape, BF16),
            pltpu.VMEM(back.shape, BF16),
            pltpu.VMEM(gmat.shape, BF16),
            pltpu.VMEM(dmat.shape, BF16),
            pltpu.VMEM((ELEMS, 2, ROWS, LANES), F32),
            pltpu.VMEM((GROUPS, 2, 2, ROWS, LANES), F32),
            pltpu.VMEM((4 * ROWS, MODES), BF16),
            pltpu.VMEM((4 * ROWS, PLANES), BF16),
            pltpu.VMEM((2, PLANES // CHUNK, 16, CHUNK), F32),
            pltpu.VMEM((2, 4, ROWS, LANES), F32),
            pltpu.VMEM((4, ELEMS, ROWS, LANES), F32),
            pltpu.VMEM((RAD, ROWS, LANES), F32),
            pltpu.VMEM((2, GROUPS, 2, ROWS, LANES), F32),
            pltpu.VMEM((ELEMS, 2, ROWS, LANES), F32),
            pltpu.VMEM((2, ELEMS, ROWS, LANES), F32),
            pltpu.VMEM((2, ELEMS, ROWS, LANES), F32),
            pltpu.VMEM((2, 2, 2, RAD, 16, LANES), F32),
            pltpu.VMEM((2, 2, 2, RAD, 16, LANES), F32),
            pltpu.VMEM((2, 4, 8, LANES), F32),
            pltpu.VMEM((2, 8, LANES), F32),
            pltpu.VMEM((ZRING, 8, LANES), F32),
            pltpu.VMEM((size_y, 8, LANES), F32),
            dma((7,)),
            dma((2, GROUPS)),
            dma((2, GROUPS)),
            dma((4,)),
            dma((2, GROUPS)),
            dma((2, GROUPS)),
            dma((2, 2, 2)),
            dma((2, 2, 2)),
            dma((ZRING,)),
            dma((ZRING,)),
            dma((size_y,)),
            dma((size_y,)),
        ],
        compiler_params=pltpu.CompilerParams(
            collective_id=0, has_side_effects=True, vmem_limit_bytes=56 * 2**20
        ),
    )(
        vel_x.reshape(rows, LANES),
        vel_y.reshape(rows, LANES),
        metrics,
        slot_order,
        jnp.asarray(there),
        jnp.asarray(back),
        jnp.asarray(gmat),
        jnp.asarray(dmat),
    )
    out_x, out_y = pl.pallas_call(
        scatter_kernel,
        out_shape=[jax.ShapeDtypeStruct((rows, LANES), F32)] * 2,
        in_specs=[smem, vmem],
        out_specs=[vmem, vmem],
        compiler_params=pltpu.CompilerParams(vmem_limit_bytes=32 * 2**20),
    )(slot_order, grid)
    shape = (NODES, ELEMS, LANES)
    return out_x.reshape(shape), out_y.reshape(shape)


def solution(mesh):
    placed = (P(None, "elem", "mode"), P(None, "elem", "mode"), P(None, None, "elem"), P("elem"))
    return jax.shard_map(
        functools.partial(body, mesh.shape["elem"]),
        mesh=mesh,
        in_specs=placed,
        out_specs=(P(None, "elem", "mode"), P(None, "elem", "mode")),
        check_vma=False,
    )
```

```python
import functools
import math

import jax
import jax.numpy as jnp
import ml_dtypes
import numpy as np
from jax import lax
from jax.experimental import pallas as pl
from jax.experimental.pallas import tpu as pltpu
from jax.sharding import PartitionSpec as P

ORDER = 8
NP = ORDER + 1
NODES = NP * NP
ROWS = 88
KROWS = 96
EDGE = NODES - NP
RAD = 4
AZ = 4
ELEMS = 16
MODES = 1024
PLANES = 1536
LANES = 128
CHUNK = 256
GROUPS = 8
ZRING = 8
SIGMA = 2.0
WAVE = 64.0
MESH = pl.DeviceIdType.MESH
F32 = jnp.float32
BF16 = jnp.bfloat16


def legendre_value(order, point):
    previous = 1.0
    current = point
    for degree in range(2, order + 1):
        previous, current = (
            current,
            ((2 * degree - 1) * point * current - (degree - 1) * previous) / degree,
        )
    return (current, previous)


def gll_matrix(order):
    points = []
    for index in range(order + 1):
        point = -math.cos(math.pi * index / order)
        for sweep in range(100):
            high, lower = legendre_value(order, point)
            point = point - (point * high - lower) / ((order + 1) * high)
        points.append(point)
    points[0] = -1.0
    points[order] = 1.0
    values = [legendre_value(order, point)[0] for point in points]
    number = order + 1
    matrix = np.zeros((number, number))
    for row_index in range(number):
        for col_index in range(number):
            if row_index != col_index:
                matrix[row_index, col_index] = values[row_index] / (
                    values[col_index] * (points[row_index] - points[col_index])
                )
    matrix[0, 0] = -order * (order + 1) / 4.0
    matrix[order, order] = order * (order + 1) / 4.0
    return matrix


def halves(array):
    array = np.asarray(array, np.float32)
    high = array.astype(ml_dtypes.bfloat16)
    low = (array - high.astype(np.float32)).astype(ml_dtypes.bfloat16)
    return high, low


@functools.lru_cache(maxsize=None)
def constants():
    wave = np.arange(MODES)
    freq = (wave + 1) // 2
    phase = freq[:, None] * np.arange(PLANES)[None, :] % PLANES
    angle = 2.0 * np.pi / PLANES * phase
    table = np.where((wave % 2 == 0)[:, None], np.cos(angle), np.sin(angle))
    table = table * np.where(wave == 0, math.sqrt(1.0 / PLANES), math.sqrt(2.0 / PLANES))[:, None]
    high, low = halves(table)
    there = np.stack([high, low]).reshape(2, MODES, PLANES // CHUNK, CHUNK).transpose(0, 2, 1, 3)
    back = np.stack([high.T, low.T]).reshape(2, PLANES, MODES // CHUNK, CHUNK).transpose(0, 2, 1, 3)
    dmat = gll_matrix(ORDER).astype(np.float32)
    eye = np.eye(NP, dtype=np.float32)
    grad = np.zeros((2, ROWS, ROWS), np.float32)
    grad[0, :NODES, :NODES] = np.kron(dmat, eye)
    grad[1, :NODES, :NODES] = np.kron(eye, dmat)
    ghigh, glow = halves(grad.reshape(2 * ROWS, ROWS))
    gmat = np.zeros((4 * ROWS, 2 * KROWS), ml_dtypes.bfloat16)
    gmat[: 2 * ROWS, :ROWS] = ghigh
    gmat[: 2 * ROWS, KROWS : KROWS + ROWS] = ghigh
    gmat[2 * ROWS :, :ROWS] = glow
    dhigh, dlow = halves(grad.transpose(2, 0, 1).reshape(ROWS, 2 * ROWS))
    dmat2 = np.zeros((2 * KROWS, 2 * ROWS), ml_dtypes.bfloat16)
    dmat2[:ROWS] = dhigh
    dmat2[KROWS : KROWS + ROWS] = dlow
    return np.ascontiguousarray(there), np.ascontiguousarray(back), gmat, dmat2


def split(value):
    high = value.astype(BF16)
    return high, (value - high.astype(F32)).astype(BF16)


def split_rows(value):
    high = value.astype(BF16).astype(F32)
    gap = jnp.zeros((KROWS - ROWS, value.shape[1]), F32)
    return jnp.concatenate([high, gap, value - high, gap], axis=0).astype(BF16)


def mm(a, b):
    return jnp.dot(a, b, preferred_element_type=F32)


def fold(value):
    total = jnp.sum(value.reshape(ROWS // 8, 8, value.shape[1]), axis=0)
    out = total[:, :LANES]
    for at in range(1, value.shape[1] // LANES):
        out = out + total[:, at * LANES : (at + 1) * LANES]
    return out


def position(rank, second):
    row, side = rank // 2, rank % 2
    return row * AZ + (1 + side if second else (AZ - 1) * side)


def kernel(
    size_e,
    velx_hbm,
    vely_hbm,
    met_hbm,
    slots,
    there_hbm,
    back_hbm,
    gmat_hbm,
    dmat_hbm,
    out,
    vel,
    met,
    there,
    back,
    gmat,
    dmat,
    snd,
    rv,
    act,
    wave,
    pgeo,
    geo,
    wts,
    ret,
    rv2,
    bf,
    yf,
    hs,
    hr,
    acc,
    part,
    gat_z,
    gat_y,
    in_sem,
    s1,
    r1,
    own,
    s2,
    r2,
    hsem,
    hrem,
    as_z,
    ar_z,
    as_y,
    ar_y,
):
    me_e = lax.axis_index("elem")
    me = lax.axis_index("mode")
    chip, core = me // 2, me % 2
    zed, why = me_e % ZRING, me_e // ZRING
    size_y = size_e // ZRING
    left = (me_e + size_e - 1) % size_e
    right = (me_e + 1) % size_e
    peers = [
        (((chip + dc) % 4) * 2 + (core + cc) % 2)
        for dc, cc in ((2, 0), (2, 1), (1, 0), (3, 0), (1, 1), (3, 1), (0, 1))
    ]
    z_peers = [why * ZRING + (zed + k) % ZRING for k in (4, 3, 5, 2, 6, 1, 7)]
    y_hops = sorted(range(1, size_y), key=lambda k: -min(k, size_y - k))
    y_peers = [((why + k) % size_y) * ZRING + zed for k in y_hops]

    loads = [
        pltpu.make_async_copy(velx_hbm, vel.at[0], in_sem.at[0]),
        pltpu.make_async_copy(vely_hbm, vel.at[1], in_sem.at[1]),
        pltpu.make_async_copy(met_hbm, met, in_sem.at[2]),
        pltpu.make_async_copy(gmat_hbm, gmat, in_sem.at[3]),
        pltpu.make_async_copy(dmat_hbm, dmat, in_sem.at[4]),
        pltpu.make_async_copy(there_hbm, there, in_sem.at[5]),
        pltpu.make_async_copy(back_hbm, back, in_sem.at[6]),
    ]
    for copy in loads[:5]:
        copy.start()

    tail = jnp.zeros((2, 8, LANES), F32)
    for p in range(ELEMS):
        snd[p, :, ROWS - 8 :, :] = tail
        rv[p // 2, p % 2, :, ROWS - 8 :, :] = tail
        rv2[p, :, ROWS - 8 :, :] = tail

    barrier = pltpu.get_barrier_semaphore()
    for peer in peers:
        pl.semaphore_signal(barrier, inc=1, device_id=(me_e, peer), device_id_type=MESH)
    for peer in z_peers + y_peers + [left, right]:
        pl.semaphore_signal(barrier, inc=1, device_id=(peer, me), device_id_type=MESH)

    pl.semaphore_wait(barrier, len(peers) + len(z_peers) + len(y_peers) + 2)

    loads[0].wait()
    loads[1].wait()

    def gather(p):
        slot = slots[p]
        for c in range(2):
            snd[p, c, 0:NODES, :] = vel[c, pl.ds(slot, NODES, stride=ELEMS), :]

    sends = []
    arrivals = [[], []]
    locals_ = []
    for e in range(2):
        for k, peer in enumerate(peers):
            p = position(peer, e)
            gather(p)
            copy = pltpu.make_async_remote_copy(
                src_ref=snd.at[p, :, pl.ds(0, NODES)],
                dst_ref=rv.at[me, e, :, pl.ds(0, NODES)],
                send_sem=s1.at[e, k],
                recv_sem=r1.at[e, me],
                device_id=(me_e, peer),
                device_id_type=MESH,
            )
            copy.start()
            sends.append(copy)
        p = position(me, e)
        gather(p)
        copy = pltpu.make_async_copy(
            snd.at[p, :, pl.ds(0, NODES)], rv.at[me, e, :, pl.ds(0, NODES)], own.at[e]
        )
        copy.start()
        locals_.append(copy)
        for k, peer in enumerate(peers):
            arrivals[e].append(
                pltpu.make_async_remote_copy(
                    src_ref=snd.at[0, :, pl.ds(0, NODES)],
                    dst_ref=rv.at[peer, e, :, pl.ds(0, NODES)],
                    send_sem=s1.at[e, k],
                    recv_sem=r1.at[e, peer],
                    device_id=(me_e, peer),
                    device_id_type=MESH,
                )
            )

    loads[5].start()
    loads[6].start()

    loads[2].wait()
    loads[3].wait()
    loads[4].wait()
    row16 = lax.broadcasted_iota(jnp.int32, (ELEMS, LANES), 0)

    def picker(p):
        return jnp.where(row16 == slots[p], 1.0, 0.0).astype(BF16)

    def spread(factors, pick):
        gap = jnp.zeros((ELEMS, ROWS - NODES), F32)
        full = jnp.concatenate([factors, gap], axis=1).T
        high = full.astype(BF16)
        rest = full - high.astype(F32)
        mid = rest.astype(BF16)
        low = (rest - mid.astype(F32)).astype(BF16)
        return mm(high, pick) + mm(mid, pick) + mm(low, pick)

    mine = jnp.concatenate([picker(position(me, 0)), picker(position(me, 1))], axis=1)
    jac = spread(met[7], mine)
    for g in range(4):
        full = spread(met[g], mine) * jac
        pgeo[0, g] = full[:, :LANES]
        pgeo[1, g] = full[:, LANES:]

    def spread_row(r, carry):
        pick = jnp.concatenate([picker(r * AZ + a) for a in range(AZ)], axis=1)
        for g in range(4):
            full = spread(met[4 + g], pick)
            for a in range(AZ):
                geo[g, r * AZ + a] = full[:, a * LANES : (a + 1) * LANES]
        return carry

    lax.fori_loop(0, RAD, spread_row, 0)

    node = lax.broadcasted_iota(jnp.int32, (ROWS, LANES), 0)
    along = node % NP
    sides = jnp.where((along == 0) | (along == NP - 1), 0.5, 1.0).astype(F32)
    sides = jnp.where(node < NODES, sides, 0.0)
    first, last = node < NP, node >= EDGE
    wts[0] = jnp.where(first, 0.0, jnp.where(last, 0.5, 1.0)) * sides
    wts[1] = jnp.where(first | last, 0.5, 1.0) * sides
    wts[2] = wts[1]
    wts[3] = jnp.where(last, 0.0, jnp.where(first, 0.5, 1.0)) * sides

    lane = lax.broadcasted_iota(jnp.int32, (1, LANES), 1) + me * LANES
    freq = ((lane + 1) // 2).astype(F32) / WAVE
    lam = SIGMA + freq * freq

    acc[...] = jnp.zeros_like(acc)

    def prior(p, carry):
        twice = SIGMA * geo[3, p]
        for c in range(2):
            bf[c, p] = twice * snd[p, c]
        return carry

    lax.fori_loop(0, ELEMS, prior, 0)

    ret_sends = []
    ret_locals = [[], []]
    for e in range(2):
        for copy in arrivals[e]:
            copy.wait_recv()
        locals_[e].wait()
        for src in range(GROUPS):
            both = rv[src, e].reshape(2 * ROWS, LANES)
            high, low = split(both)
            act[0 : 2 * ROWS, src * LANES : (src + 1) * LANES] = high
            act[2 * ROWS :, src * LANES : (src + 1) * LANES] = low
        if e == 0:
            loads[5].wait()

        def planes(z, carry, e=e):
            top = mm(act[...], there[0, z])
            field = top[: 2 * ROWS] + top[2 * ROWS :] + mm(act[0 : 2 * ROWS, :], there[1, z])
            u, v = field[:ROWS], field[ROWS:]
            diff = mm(gmat[...], split_rows(jnp.concatenate([u, v], axis=1)))
            diff = diff[: 2 * ROWS] + diff[2 * ROWS :]
            m = [jnp.concatenate([pgeo[e, g]] * (CHUNK // LANES), axis=1) for g in range(4)]
            by_i = u * m[0] + v * m[2]
            by_j = u * m[1] + v * m[3]
            for c in range(2):
                cols = slice(c * CHUNK, (c + 1) * CHUNK)
                prod = by_i * diff[:ROWS, cols] + by_j * diff[ROWS:, cols]
                at = pl.ds(pl.multiple_of(z * CHUNK, CHUNK), CHUNK)
                wave[c * 2 * KROWS : (c + 1) * 2 * KROWS, at] = split_rows(prod)
            return carry

        lax.fori_loop(0, PLANES // CHUNK, planes, 0, unroll=3)
        if e == 0:
            loads[6].wait()

        for c in range(2):
            for step, dc in enumerate((2, 1, 3, 0)):
                n = (chip + dc) % 4
                top = mm(wave[c * 2 * KROWS : (c + 1) * 2 * KROWS, :], back[0, n])
                low = mm(wave[c * 2 * KROWS : c * 2 * KROWS + KROWS, :], back[1, n])
                hat = top[:ROWS] + top[KROWS : KROWS + ROWS] + low[:ROWS]
                for half in range(2):
                    ret[e, n * 2 + half, c] = hat[:, half * LANES : (half + 1) * LANES]
                for cc in range(2):
                    peer = n * 2 + (core + cc) % 2
                    src = ret.at[e, peer, c, pl.ds(0, NODES)]
                    dst = rv2.at[position(me, e), c, pl.ds(0, NODES)]
                    if dc == 0 and cc == 0:
                        copy = pltpu.make_async_copy(src, dst, own.at[2 + 2 * e + c])
                        ret_locals[c].append(copy)
                    else:
                        copy = pltpu.make_async_remote_copy(
                            src_ref=src,
                            dst_ref=dst,
                            send_sem=s2.at[e, c, step * 2 + cc],
                            recv_sem=r2.at[e, c, me],
                            device_id=(me_e, peer),
                            device_id_type=MESH,
                        )
                        ret_sends.append(copy)
                    copy.start()

    def wait_returns(e, c):
        for peer in peers:
            pltpu.make_async_remote_copy(
                src_ref=ret.at[e, 0, c, pl.ds(0, NODES)],
                dst_ref=rv2.at[position(peer, e), c, pl.ds(0, NODES)],
                send_sem=s2.at[e, c, 0],
                recv_sem=r2.at[e, c, peer],
                device_id=(me_e, peer),
                device_id_type=MESH,
            ).wait_recv()
        ret_locals[c][e].wait()

    halo_sends = []

    def radial(field, c, cols):
        for a in cols:
            for r in range(RAD - 1):
                up, down = r * AZ + a, (r + 1) * AZ + a
                joined = field[c, up, EDGE : EDGE + 8] + field[c, down, 0:8]
                corner = field[c, up, EDGE + 8 : NODES] + field[c, down, 8:NP]
                field[c, up, EDGE : EDGE + 8] = joined
                field[c, down, 0:8] = joined
                field[c, up, EDGE + 8 : NODES] = corner
                field[c, down, 8:NP] = corner
            field[c, a, 0:8] = jnp.zeros((8, LANES), F32)
            field[c, a, 8:NP] = jnp.zeros((1, LANES), F32)
            end = (RAD - 1) * AZ + a
            field[c, end, EDGE : EDGE + 8] = jnp.zeros((8, LANES), F32)
            field[c, end, EDGE + 8 : NODES] = jnp.zeros((1, LANES), F32)

    first_edge = pl.ds(0, NP, stride=NP)
    last_edge = pl.ds(NP - 1, NP, stride=NP)

    def rims_start(field, c, which):
        for r in range(RAD):
            hs[which, c, 0, r, 0:NP] = field[c, r * AZ, first_edge, :]
            hs[which, c, 1, r, 0:NP] = field[c, r * AZ + AZ - 1, last_edge, :]
        copies = []
        for side, peer in ((0, left), (1, right)):
            copy = pltpu.make_async_remote_copy(
                src_ref=hs.at[which, c, side, :, pl.ds(0, NP)],
                dst_ref=hr.at[which, c, side, :, pl.ds(0, NP)],
                send_sem=hsem.at[which, c, side],
                recv_sem=hrem.at[which, c, side],
                device_id=(peer, me),
                device_id_type=MESH,
            )
            copy.start()
            copies.append(copy)
        halo_sends.extend(copies)
        return copies

    def joints(field, c):
        for r in range(RAD):
            for a in range(AZ - 1):
                p = r * AZ + a
                shared = field[c, p, last_edge, :] + field[c, p + 1, first_edge, :]
                field[c, p, last_edge, :] = shared
                field[c, p + 1, first_edge, :] = shared

    def rims_finish(field, c, which, copies):
        for copy in copies:
            copy.wait_recv()
        for r in range(RAD):
            p = r * AZ + AZ - 1
            field[c, p, last_edge, :] = field[c, p, last_edge, :] + hr[which, c, 0, r, 0:NP]
            p = r * AZ
            field[c, p, first_edge, :] = field[c, p, first_edge, :] + hr[which, c, 1, r, 0:NP]

    def pair(ref, c, p0, p1):
        return jnp.concatenate([ref[c, p0], ref[c, p1]], axis=1)

    def fluxes(x, p0, p1):
        diff = mm(gmat[...], split_rows(x))
        diff = diff[: 2 * ROWS] + diff[2 * ROWS :]
        x_i, x_j = diff[:ROWS], diff[ROWS:]
        g = [pair(geo, k, p0, p1) for k in range(4)]
        return x_i, x_j, g[0] * x_i + g[1] * x_j, g[1] * x_i + g[2] * x_j, g[3]

    lam2 = jnp.concatenate([lam, lam], axis=1)

    def weights(r):
        return jnp.concatenate([wts[r], wts[r]], axis=1)

    def apply(c, cols):
        def step(r, carry):
            p0, p1 = r * AZ + cols[0], r * AZ + cols[1]
            x = pair(bf, c, p0, p1)
            x_i, x_j, f_i, f_j, jw = fluxes(x, p0, p1)
            high, low = split(jnp.concatenate([f_i, f_j], axis=0))
            top = mm(dmat[...], high)
            y = top[:ROWS] + top[KROWS : KROWS + ROWS] + mm(dmat[0:KROWS, :], low)[:ROWS]
            y = y + lam2 * jw * x
            yf[c, p0] = y[:, :LANES]
            yf[c, p1] = y[:, LANES:]
            acc[c, 0] = acc[c, 0] + fold(x * x * weights(r))
            acc[c, 1] = acc[c, 1] + fold(x * y)
            return carry

        lax.fori_loop(0, RAD, step, 0, unroll=4)

    def energy(c, cols):
        def step(r, carry):
            p0, p1 = r * AZ + cols[0], r * AZ + cols[1]
            y = pair(yf, c, p0, p1)
            y_i, y_j, f_i, f_j, jw = fluxes(y, p0, p1)
            acc[c, 2] = acc[c, 2] + fold(y * y * weights(r))
            acc[c, 3] = acc[c, 3] + fold(f_i * y_i + f_j * y_j + lam2 * jw * y * y)
            return carry

        lax.fori_loop(0, RAD, step, 0, unroll=4)

    def rhs(c, cols):
        for r in range(RAD):
            for a in cols:
                p = r * AZ + a
                bf[c, p] = bf[c, p] - rv2[p, c]
        radial(bf, c, cols)

    inside, outside = (1, 2), (0, AZ - 1)
    b_flights, y_flights = [], []
    for c in range(2):
        wait_returns(0, c)
        rhs(c, outside)
        b_flights.append(rims_start(bf, c, 0))
    for c in range(2):
        wait_returns(1, c)
        rhs(c, inside)
        joints(bf, c)
        rims_finish(bf, c, 0, b_flights[c])
        apply(c, outside)
        radial(yf, c, outside)
        y_flights.append(rims_start(yf, c, 1))
        apply(c, inside)
        radial(yf, c, inside)
        joints(yf, c)
    energy(0, inside)
    rims_finish(yf, 0, 1, y_flights[0])
    energy(0, outside)
    energy(1, inside)
    rims_finish(yf, 1, 1, y_flights[1])
    energy(1, outside)

    sums = jnp.concatenate(
        [jnp.sum(acc[c, k], axis=0, keepdims=True) for c in range(2) for k in range(4)], axis=0
    )

    def exchange(value, slot, group, send_sem, recv_sem, ranks, mine_at, to_device):
        part[slot] = value
        copies = []
        for k, (peer, at) in enumerate(ranks):
            copy = pltpu.make_async_remote_copy(
                src_ref=part.at[slot],
                dst_ref=group.at[mine_at],
                send_sem=send_sem.at[k],
                recv_sem=recv_sem.at[mine_at],
                device_id=(peer, me),
                device_id_type=MESH,
            )
            copy.start()
            copies.append(copy)
        total = value
        for k, (peer, at) in enumerate(ranks):
            pltpu.make_async_remote_copy(
                src_ref=part.at[slot],
                dst_ref=group.at[at],
                send_sem=send_sem.at[k],
                recv_sem=recv_sem.at[at],
                device_id=(peer, me),
                device_id_type=MESH,
            ).wait_recv()
        group[mine_at] = value
        total = group[0]
        for at in range(1, len(ranks) + 1):
            total = total + group[at]
        return total, copies

    z_ranks = [(peer, peer % ZRING) for peer in z_peers]
    y_ranks = [(peer, peer // ZRING) for peer in y_peers]
    sums, more = exchange(sums, 0, gat_z, as_z, ar_z, z_ranks, zed, None)
    halo_sends.extend(more)
    if y_ranks:
        sums, more = exchange(sums, 1, gat_y, as_y, ar_y, y_ranks, why, None)
        halo_sends.extend(more)

    for c in range(2):
        m0, m1, m2, m3 = (sums[c * 4 + k : c * 4 + k + 1] for k in range(4))
        alpha = m0 / m1
        grown = alpha * alpha * m2 - m0
        scale = 1.0 + grown / m0
        below = scale * scale * m1 - 2.0 * scale * alpha * m2 + alpha * alpha * m3
        beyond = grown / below
        on_b = alpha + beyond * scale
        on_y = -beyond * alpha

        def combine(p, carry, c=c, on_b=on_b, on_y=on_y):
            out[c, p] = on_b * bf[c, p] + on_y * yf[c, p]
            return carry

        lax.fori_loop(0, ELEMS, combine, 0)

    for copy in sends + ret_sends + halo_sends:
        copy.wait_send()


def scatter_kernel(slots, grid, out_x, out_y):
    for p in range(ELEMS):
        slot = slots[p]
        out_x[pl.ds(slot, NODES, stride=ELEMS), :] = grid[0, p, 0:NODES]
        out_y[pl.ds(slot, NODES, stride=ELEMS), :] = grid[1, p, 0:NODES]


def body(size_e, vel_x, vel_y, metrics, slot_order):
    there, back, gmat, dmat = constants()
    any_space = pl.BlockSpec(memory_space=pl.ANY)
    vmem = pl.BlockSpec(memory_space=pltpu.VMEM)
    smem = pl.BlockSpec(memory_space=pltpu.SMEM)
    dma = pltpu.SemaphoreType.DMA
    size_y = size_e // ZRING
    rows = NODES * ELEMS
    grid = pl.pallas_call(
        functools.partial(kernel, size_e),
        out_shape=pltpu.VMEM((2, ELEMS, ROWS, LANES), F32),
        in_specs=[any_space] * 3 + [smem] + [any_space] * 4,
        out_specs=vmem,
        scratch_shapes=[
            pltpu.VMEM((2, rows, LANES), F32),
            pltpu.VMEM((8, ELEMS, NODES), F32),
            pltpu.VMEM(there.shape, BF16),
            pltpu.VMEM(back.shape, BF16),
            pltpu.VMEM(gmat.shape, BF16),
            pltpu.VMEM(dmat.shape, BF16),
            pltpu.VMEM((ELEMS, 2, ROWS, LANES), F32),
            pltpu.VMEM((GROUPS, 2, 2, ROWS, LANES), F32),
            pltpu.VMEM((4 * ROWS, MODES), BF16),
            pltpu.VMEM((4 * KROWS, PLANES), BF16),
            pltpu.VMEM((2, 4, ROWS, LANES), F32),
            pltpu.VMEM((4, ELEMS, ROWS, LANES), F32),
            pltpu.VMEM((RAD, ROWS, LANES), F32),
            pltpu.VMEM((2, GROUPS, 2, ROWS, LANES), F32),
            pltpu.VMEM((ELEMS, 2, ROWS, LANES), F32),
            pltpu.VMEM((2, ELEMS, ROWS, LANES), F32),
            pltpu.VMEM((2, ELEMS, ROWS, LANES), F32),
            pltpu.VMEM((2, 2, 2, RAD, 16, LANES), F32),
            pltpu.VMEM((2, 2, 2, RAD, 16, LANES), F32),
            pltpu.VMEM((2, 4, 8, LANES), F32),
            pltpu.VMEM((2, 8, LANES), F32),
            pltpu.VMEM((ZRING, 8, LANES), F32),
            pltpu.VMEM((size_y, 8, LANES), F32),
            dma((7,)),
            dma((2, GROUPS)),
            dma((2, GROUPS)),
            dma((6,)),
            dma((2, 2, GROUPS)),
            dma((2, 2, GROUPS)),
            dma((2, 2, 2)),
            dma((2, 2, 2)),
            dma((ZRING,)),
            dma((ZRING,)),
            dma((size_y,)),
            dma((size_y,)),
        ],
        compiler_params=pltpu.CompilerParams(
            collective_id=0, has_side_effects=True, vmem_limit_bytes=56 * 2**20
        ),
    )(
        vel_x.reshape(rows, LANES),
        vel_y.reshape(rows, LANES),
        metrics.transpose(0, 2, 1),
        slot_order,
        jnp.asarray(there),
        jnp.asarray(back),
        jnp.asarray(gmat),
        jnp.asarray(dmat),
    )
    out_x, out_y = pl.pallas_call(
        scatter_kernel,
        out_shape=[jax.ShapeDtypeStruct((rows, LANES), F32)] * 2,
        in_specs=[smem, vmem],
        out_specs=[vmem, vmem],
        compiler_params=pltpu.CompilerParams(vmem_limit_bytes=32 * 2**20),
    )(slot_order, grid)
    shape = (NODES, ELEMS, LANES)
    return out_x.reshape(shape), out_y.reshape(shape)


def solution(mesh):
    placed = (P(None, "elem", "mode"), P(None, "elem", "mode"), P(None, None, "elem"), P("elem"))
    return jax.shard_map(
        functools.partial(body, mesh.shape["elem"]),
        mesh=mesh,
        in_specs=placed,
        out_specs=(P(None, "elem", "mode"), P(None, "elem", "mode")),
        check_vma=False,
    )
```

```python
import functools
import math

import jax
import jax.numpy as jnp
import ml_dtypes
import numpy as np
from jax import lax
from jax.experimental import pallas as pl
from jax.experimental.pallas import tpu as pltpu
from jax.sharding import PartitionSpec as P

ORDER = 8
NP = ORDER + 1
NODES = NP * NP
ROWS = 88
KROWS = 96
EDGE = NODES - NP
RAD = 4
AZ = 4
ELEMS = 16
MODES = 1024
PLANES = 1536
LANES = 128
CHUNK = 256
GROUPS = 8
ZRING = 8
SIGMA = 2.0
WAVE = 64.0
MESH = pl.DeviceIdType.MESH
F32 = jnp.float32
BF16 = jnp.bfloat16


def legendre_value(order, point):
    previous = 1.0
    current = point
    for degree in range(2, order + 1):
        previous, current = (
            current,
            ((2 * degree - 1) * point * current - (degree - 1) * previous) / degree,
        )
    return (current, previous)


def gll_matrix(order):
    points = []
    for index in range(order + 1):
        point = -math.cos(math.pi * index / order)
        for sweep in range(100):
            high, lower = legendre_value(order, point)
            point = point - (point * high - lower) / ((order + 1) * high)
        points.append(point)
    points[0] = -1.0
    points[order] = 1.0
    values = [legendre_value(order, point)[0] for point in points]
    number = order + 1
    matrix = np.zeros((number, number))
    for row_index in range(number):
        for col_index in range(number):
            if row_index != col_index:
                matrix[row_index, col_index] = values[row_index] / (
                    values[col_index] * (points[row_index] - points[col_index])
                )
    matrix[0, 0] = -order * (order + 1) / 4.0
    matrix[order, order] = order * (order + 1) / 4.0
    return matrix


def halves(array):
    array = np.asarray(array, np.float32)
    high = array.astype(ml_dtypes.bfloat16)
    low = (array - high.astype(np.float32)).astype(ml_dtypes.bfloat16)
    return high, low


@functools.lru_cache(maxsize=None)
def constants():
    wave = np.arange(MODES)
    freq = (wave + 1) // 2
    phase = freq[:, None] * np.arange(PLANES)[None, :] % PLANES
    angle = 2.0 * np.pi / PLANES * phase
    table = np.where((wave % 2 == 0)[:, None], np.cos(angle), np.sin(angle))
    table = table * np.where(wave == 0, math.sqrt(1.0 / PLANES), math.sqrt(2.0 / PLANES))[:, None]
    high, low = halves(table)
    there = np.stack([high, low]).reshape(2, MODES, PLANES // CHUNK, CHUNK).transpose(0, 2, 1, 3)
    back = np.stack([high.T, low.T]).reshape(2, PLANES, MODES // CHUNK, CHUNK).transpose(0, 2, 1, 3)
    dmat = gll_matrix(ORDER).astype(np.float32)
    eye = np.eye(NP, dtype=np.float32)
    grad = np.zeros((2, ROWS, ROWS), np.float32)
    grad[0, :NODES, :NODES] = np.kron(dmat, eye)
    grad[1, :NODES, :NODES] = np.kron(eye, dmat)
    ghigh, glow = halves(grad.reshape(2 * ROWS, ROWS))
    gmat = np.zeros((4 * ROWS, 2 * KROWS), ml_dtypes.bfloat16)
    gmat[: 2 * ROWS, :ROWS] = ghigh
    gmat[: 2 * ROWS, KROWS : KROWS + ROWS] = ghigh
    gmat[2 * ROWS :, :ROWS] = glow
    dhigh, dlow = halves(grad.transpose(2, 0, 1).reshape(ROWS, 2 * ROWS))
    dmat2 = np.zeros((2 * KROWS, 2 * ROWS), ml_dtypes.bfloat16)
    dmat2[:ROWS] = dhigh
    dmat2[KROWS : KROWS + ROWS] = dlow
    return np.ascontiguousarray(there), np.ascontiguousarray(back), gmat, dmat2


def split(value):
    high = value.astype(BF16)
    return high, (value - high.astype(F32)).astype(BF16)


def split_rows(value):
    high = value.astype(BF16).astype(F32)
    gap = jnp.zeros((KROWS - ROWS, value.shape[1]), F32)
    return jnp.concatenate([high, gap, value - high, gap], axis=0).astype(BF16)


def mm(a, b):
    return jnp.dot(a, b, preferred_element_type=F32)


def fold(value):
    total = jnp.sum(value.reshape(ROWS // 8, 8, value.shape[1]), axis=0)
    out = total[:, :LANES]
    for at in range(1, value.shape[1] // LANES):
        out = out + total[:, at * LANES : (at + 1) * LANES]
    return out


def position(rank, second):
    row, side = rank // 2, rank % 2
    return row * AZ + (1 + side if second else (AZ - 1) * side)


def kernel(
    size_e,
    velx_hbm,
    vely_hbm,
    met_hbm,
    slots,
    there_hbm,
    back_hbm,
    gmat_hbm,
    dmat_hbm,
    out_x,
    out_y,
    vel,
    met,
    there,
    back,
    gmat,
    dmat,
    snd,
    rv,
    act,
    wave,
    pgeo,
    geo,
    wts,
    ret,
    rv2,
    bf,
    yf,
    hs,
    hr,
    acc,
    part,
    gat,
    in_sem,
    s1,
    r1,
    own,
    s2,
    r2,
    hsem,
    hrem,
    as_all,
    ar_all,
    known,
    inverse,
    esnd,
    ercv,
    es,
    er,
):
    outs = (out_x, out_y)
    me_e = lax.axis_index("elem")
    me = lax.axis_index("mode")
    chip, core = me // 2, me % 2
    zed, why = me_e % ZRING, me_e // ZRING
    size_y = size_e // ZRING
    left = (me_e + size_e - 1) % size_e
    right = (me_e + 1) % size_e
    peers = [
        (((chip + dc) % 4) * 2 + (core + cc) % 2)
        for dc, cc in ((2, 0), (2, 1), (1, 0), (3, 0), (1, 1), (3, 1), (0, 1))
    ]
    z_peers = [why * ZRING + (zed + k) % ZRING for k in (4, 3, 5, 2, 6, 1, 7)]
    y_peers = [((why + k) % size_y) * ZRING + zed for k in range(1, size_y)]

    def hops(step):
        return min(step[0], size_y - step[0]) + min(step[1], ZRING - step[1])

    steps = [(dy, dz) for dy in range(size_y) for dz in range(ZRING) if dy or dz]
    all_peers = [
        ((why + dy) % size_y) * ZRING + (zed + dz) % ZRING
        for dy, dz in sorted(steps, key=lambda step: -hops(step))
    ]

    loads = [
        pltpu.make_async_copy(velx_hbm, vel.at[0], in_sem.at[0]),
        pltpu.make_async_copy(vely_hbm, vel.at[1], in_sem.at[1]),
        pltpu.make_async_copy(met_hbm, met, in_sem.at[2]),
        pltpu.make_async_copy(gmat_hbm, gmat, in_sem.at[3]),
        pltpu.make_async_copy(dmat_hbm, dmat, in_sem.at[4]),
        pltpu.make_async_copy(there_hbm, there, in_sem.at[5]),
        pltpu.make_async_copy(back_hbm, back, in_sem.at[6]),
    ]
    for copy in loads[:5]:
        copy.start()

    tail = jnp.zeros((2, 8, LANES), F32)
    for p in range(ELEMS):
        snd[p, :, ROWS - 8 :, :] = tail
        rv[p // 2, p % 2, :, ROWS - 8 :, :] = tail
        rv2[p, :, ROWS - 8 :, :] = tail

    barrier = pltpu.get_barrier_semaphore()
    for peer in peers:
        pl.semaphore_signal(barrier, inc=1, device_id=(me_e, peer), device_id_type=MESH)
    for peer in z_peers + y_peers + [left, right]:
        pl.semaphore_signal(barrier, inc=1, device_id=(peer, me), device_id_type=MESH)

    pl.semaphore_wait(barrier, len(peers) + len(z_peers) + len(y_peers) + 2)

    for peer in y_peers:
        pl.semaphore_signal(known, inc=1, device_id=(peer, me), device_id_type=MESH)

    loads[0].wait()
    loads[1].wait()

    def gather(p):
        slot = slots[p]
        for c in range(2):
            snd[p, c, 0:NODES, :] = vel[c, pl.ds(slot, NODES, stride=ELEMS), :]

    sends = []
    arrivals = [[], []]
    locals_ = []
    for e in range(2):
        for k, peer in enumerate(peers):
            p = position(peer, e)
            gather(p)
            copy = pltpu.make_async_remote_copy(
                src_ref=snd.at[p, :, pl.ds(0, NODES)],
                dst_ref=rv.at[me, e, :, pl.ds(0, NODES)],
                send_sem=s1.at[e, k],
                recv_sem=r1.at[e, me],
                device_id=(me_e, peer),
                device_id_type=MESH,
            )
            copy.start()
            sends.append(copy)
        p = position(me, e)
        gather(p)
        copy = pltpu.make_async_copy(
            snd.at[p, :, pl.ds(0, NODES)], rv.at[me, e, :, pl.ds(0, NODES)], own.at[e]
        )
        copy.start()
        locals_.append(copy)
        for k, peer in enumerate(peers):
            arrivals[e].append(
                pltpu.make_async_remote_copy(
                    src_ref=snd.at[0, :, pl.ds(0, NODES)],
                    dst_ref=rv.at[peer, e, :, pl.ds(0, NODES)],
                    send_sem=s1.at[e, k],
                    recv_sem=r1.at[e, peer],
                    device_id=(me_e, peer),
                    device_id_type=MESH,
                )
            )

    loads[5].start()
    loads[6].start()

    loads[2].wait()
    loads[3].wait()
    loads[4].wait()
    row16 = lax.broadcasted_iota(jnp.int32, (ELEMS, LANES), 0)

    def picker(p):
        return jnp.where(row16 == slots[p], 1.0, 0.0).astype(BF16)

    def spread(factors, pick):
        gap = jnp.zeros((ELEMS, ROWS - NODES), F32)
        full = jnp.concatenate([factors, gap], axis=1).T
        high = full.astype(BF16)
        rest = full - high.astype(F32)
        mid = rest.astype(BF16)
        low = (rest - mid.astype(F32)).astype(BF16)
        return mm(high, pick) + mm(mid, pick) + mm(low, pick)

    mine = jnp.concatenate([picker(position(me, 0)), picker(position(me, 1))], axis=1)
    jac = spread(met[7], mine)
    for g in range(4):
        full = spread(met[g], mine) * jac
        pgeo[0, g] = full[:, :LANES]
        pgeo[1, g] = full[:, LANES:]

    def spread_row(r, carry):
        pick = jnp.concatenate([picker(r * AZ + a) for a in range(AZ)], axis=1)
        for g in range(4):
            full = spread(met[4 + g], pick)
            for a in range(AZ):
                geo[g, r * AZ + a] = full[:, a * LANES : (a + 1) * LANES]
        return carry

    lax.fori_loop(0, RAD, spread_row, 0)

    node = lax.broadcasted_iota(jnp.int32, (ROWS, LANES), 0)
    along = node % NP
    sides = jnp.where((along == 0) | (along == NP - 1), 0.5, 1.0).astype(F32)
    sides = jnp.where(node < NODES, sides, 0.0)
    first, last = node < NP, node >= EDGE
    wts[0] = jnp.where(first, 0.0, jnp.where(last, 0.5, 1.0)) * sides
    wts[1] = jnp.where(first | last, 0.5, 1.0) * sides
    wts[2] = wts[1]
    wts[3] = jnp.where(last, 0.0, jnp.where(first, 0.5, 1.0)) * sides

    lane = lax.broadcasted_iota(jnp.int32, (1, LANES), 1) + me * LANES
    freq = ((lane + 1) // 2).astype(F32) / WAVE
    lam = SIGMA + freq * freq

    acc[...] = jnp.zeros_like(acc)

    stored = [slots[p] for p in range(ELEMS)]
    for s in range(ELEMS):
        place = jnp.int32(0)
        for p in range(1, ELEMS):
            place = jnp.where(stored[p] == s, jnp.int32(p), place)
        inverse[s] = place

    def prior(p, carry):
        twice = SIGMA * geo[3, p]
        for c in range(2):
            bf[c, p] = twice * snd[p, c]
        return carry

    lax.fori_loop(0, ELEMS, prior, 0)

    ret_sends = []
    ret_locals = [[], []]

    def send_back(e, c):
        for k, peer in enumerate(peers):
            copy = pltpu.make_async_remote_copy(
                src_ref=ret.at[e, peer, c, pl.ds(0, NODES)],
                dst_ref=rv2.at[position(me, e), c, pl.ds(0, NODES)],
                send_sem=s2.at[e, c, k],
                recv_sem=r2.at[e, c, me],
                device_id=(me_e, peer),
                device_id_type=MESH,
            )
            copy.start()
            ret_sends.append(copy)
        copy = pltpu.make_async_copy(
            ret.at[e, me, c, pl.ds(0, NODES)],
            rv2.at[position(me, e), c, pl.ds(0, NODES)],
            own.at[2 + 2 * e + c],
        )
        copy.start()
        ret_locals[c].append(copy)
    for e in range(2):
        for copy in arrivals[e]:
            copy.wait_recv()
        locals_[e].wait()
        for src in range(GROUPS):
            both = rv[src, e].reshape(2 * ROWS, LANES)
            high, low = split(both)
            act[0 : 2 * ROWS, src * LANES : (src + 1) * LANES] = high
            act[2 * ROWS :, src * LANES : (src + 1) * LANES] = low
        if e == 0:
            loads[5].wait()

        def planes(z, carry, e=e):
            top = mm(act[...], there[0, z])
            field = top[: 2 * ROWS] + top[2 * ROWS :] + mm(act[0 : 2 * ROWS, :], there[1, z])
            u, v = field[:ROWS], field[ROWS:]
            diff = mm(gmat[...], split_rows(jnp.concatenate([u, v], axis=1)))
            diff = diff[: 2 * ROWS] + diff[2 * ROWS :]
            m = [jnp.concatenate([pgeo[e, g]] * (CHUNK // LANES), axis=1) for g in range(4)]
            by_i = u * m[0] + v * m[2]
            by_j = u * m[1] + v * m[3]
            for c in range(2):
                cols = slice(c * CHUNK, (c + 1) * CHUNK)
                prod = by_i * diff[:ROWS, cols] + by_j * diff[ROWS:, cols]
                at = pl.ds(pl.multiple_of(z * CHUNK, CHUNK), CHUNK)
                wave[c * 2 * KROWS : (c + 1) * 2 * KROWS, at] = split_rows(prod)
            return carry

        lax.fori_loop(0, PLANES // CHUNK, planes, 0, unroll=3)
        if e == 0:
            loads[6].wait()

        for c in range(2):
            for step, dc in enumerate((2, 1, 3, 0)):
                n = (chip + dc) % 4
                top = mm(wave[c * 2 * KROWS : (c + 1) * 2 * KROWS, :], back[0, n])
                low = mm(wave[c * 2 * KROWS : c * 2 * KROWS + KROWS, :], back[1, n])
                hat = top[:ROWS] + top[KROWS : KROWS + ROWS] + low[:ROWS]
                for half in range(2):
                    ret[e, n * 2 + half, c] = hat[:, half * LANES : (half + 1) * LANES]
            if e == 0:
                send_back(e, c)
        if e == 1:
            shared = pl.ds((me % 2) * (NP - 1), NP, stride=NP)
            for rank in range(GROUPS):
                for c in range(2):
                    esnd[rank, c, 0:NP] = ret[1, rank, c, shared, :]
            for k, peer in enumerate(peers):
                copy = pltpu.make_async_remote_copy(
                    src_ref=esnd.at[peer, :, pl.ds(0, NP)],
                    dst_ref=ercv.at[me, :, pl.ds(0, NP)],
                    send_sem=es.at[k],
                    recv_sem=er.at[me],
                    device_id=(me_e, peer),
                    device_id_type=MESH,
                )
                copy.start()
                ret_sends.append(copy)
            for c in range(2):
                ercv[me, c, 0:NP] = esnd[me, c, 0:NP]
                send_back(e, c)

    def wait_returns(e, c):
        for peer in peers:
            pltpu.make_async_remote_copy(
                src_ref=ret.at[e, 0, c, pl.ds(0, NODES)],
                dst_ref=rv2.at[position(peer, e), c, pl.ds(0, NODES)],
                send_sem=s2.at[e, c, 0],
                recv_sem=r2.at[e, c, peer],
                device_id=(me_e, peer),
                device_id_type=MESH,
            ).wait_recv()
        ret_locals[c][e].wait()

    halo_sends = []

    def radial(field, c, cols):
        for a in cols:
            for r in range(RAD - 1):
                up, down = r * AZ + a, (r + 1) * AZ + a
                joined = field[c, up, EDGE : EDGE + 8] + field[c, down, 0:8]
                corner = field[c, up, EDGE + 8 : NODES] + field[c, down, 8:NP]
                field[c, up, EDGE : EDGE + 8] = joined
                field[c, down, 0:8] = joined
                field[c, up, EDGE + 8 : NODES] = corner
                field[c, down, 8:NP] = corner
            field[c, a, 0:8] = jnp.zeros((8, LANES), F32)
            field[c, a, 8:NP] = jnp.zeros((1, LANES), F32)
            end = (RAD - 1) * AZ + a
            field[c, end, EDGE : EDGE + 8] = jnp.zeros((8, LANES), F32)
            field[c, end, EDGE + 8 : NODES] = jnp.zeros((1, LANES), F32)

    first_edge = pl.ds(0, NP, stride=NP)
    last_edge = pl.ds(NP - 1, NP, stride=NP)

    def rims_start(field, c, which):
        for r in range(RAD):
            hs[which, c, 0, r, 0:NP] = field[c, r * AZ, first_edge, :]
            hs[which, c, 1, r, 0:NP] = field[c, r * AZ + AZ - 1, last_edge, :]
        copies = []
        for side, peer in ((0, left), (1, right)):
            copy = pltpu.make_async_remote_copy(
                src_ref=hs.at[which, c, side, :, pl.ds(0, NP)],
                dst_ref=hr.at[which, c, side, :, pl.ds(0, NP)],
                send_sem=hsem.at[which, c, side],
                recv_sem=hrem.at[which, c, side],
                device_id=(peer, me),
                device_id_type=MESH,
            )
            copy.start()
            copies.append(copy)
        halo_sends.extend(copies)
        return copies

    def joints(field, c):
        for r in range(RAD):
            for a in range(AZ - 1):
                p = r * AZ + a
                shared = field[c, p, last_edge, :] + field[c, p + 1, first_edge, :]
                field[c, p, last_edge, :] = shared
                field[c, p + 1, first_edge, :] = shared

    def rims_finish(field, c, which, copies):
        for copy in copies:
            copy.wait_recv()
        for r in range(RAD):
            p = r * AZ + AZ - 1
            field[c, p, last_edge, :] = field[c, p, last_edge, :] + hr[which, c, 0, r, 0:NP]
            p = r * AZ
            field[c, p, first_edge, :] = field[c, p, first_edge, :] + hr[which, c, 1, r, 0:NP]

    def pair(ref, c, p0, p1):
        return jnp.concatenate([ref[c, p0], ref[c, p1]], axis=1)

    def fluxes(x, p0, p1):
        diff = mm(gmat[...], split_rows(x))
        diff = diff[: 2 * ROWS] + diff[2 * ROWS :]
        x_i, x_j = diff[:ROWS], diff[ROWS:]
        g = [pair(geo, k, p0, p1) for k in range(4)]
        return x_i, x_j, g[0] * x_i + g[1] * x_j, g[1] * x_i + g[2] * x_j, g[3]

    lam2 = jnp.concatenate([lam, lam], axis=1)

    def weights(r):
        return jnp.concatenate([wts[r], wts[r]], axis=1)

    def apply(c, cols):
        def step(r, carry):
            p0, p1 = r * AZ + cols[0], r * AZ + cols[1]
            x = pair(bf, c, p0, p1)
            x_i, x_j, f_i, f_j, jw = fluxes(x, p0, p1)
            high, low = split(jnp.concatenate([f_i, f_j], axis=0))
            top = mm(dmat[...], high)
            y = top[:ROWS] + top[KROWS : KROWS + ROWS] + mm(dmat[0:KROWS, :], low)[:ROWS]
            y = y + lam2 * jw * x
            yf[c, p0] = y[:, :LANES]
            yf[c, p1] = y[:, LANES:]
            acc[c, 0] = acc[c, 0] + fold(x * x * weights(r))
            acc[c, 1] = acc[c, 1] + fold(x * y)
            return carry

        lax.fori_loop(0, RAD, step, 0, unroll=4)

    def energy(c, cols):
        def step(r, carry):
            p0, p1 = r * AZ + cols[0], r * AZ + cols[1]
            y = pair(yf, c, p0, p1)
            y_i, y_j, f_i, f_j, jw = fluxes(y, p0, p1)
            acc[c, 2] = acc[c, 2] + fold(y * y * weights(r))
            acc[c, 3] = acc[c, 3] + fold(f_i * y_i + f_j * y_j + lam2 * jw * y * y)
            return carry

        lax.fori_loop(0, RAD, step, 0, unroll=4)

    def rhs(c, cols):
        for r in range(RAD):
            for a in cols:
                p = r * AZ + a
                bf[c, p] = bf[c, p] - rv2[p, c]
        radial(bf, c, cols)

    inside, outside = (1, 2), (0, AZ - 1)
    b_flights, y_flights = [], []
    for c in range(2):
        wait_returns(0, c)
        rhs(c, outside)
        b_flights.append(rims_start(bf, c, 0))
    for peer in peers:
        pltpu.make_async_remote_copy(
            src_ref=esnd.at[peer, :, pl.ds(0, NP)],
            dst_ref=ercv.at[peer, :, pl.ds(0, NP)],
            send_sem=es.at[0],
            recv_sem=er.at[peer],
            device_id=(me_e, peer),
            device_id_type=MESH,
        ).wait_recv()

    seams = ((0, last_edge, 1, first_edge), (AZ - 1, first_edge, AZ - 2, last_edge))

    def outer_seams(c):
        for side, (outer, edge_o, inner, edge_i) in enumerate(seams):
            terms = [
                bf[c, r * AZ + inner, edge_i, :] - ercv[2 * r + side, c, 0:NP] for r in range(RAD)
            ]
            zero = jnp.zeros((1, LANES), F32)
            joins = [zero] + [terms[r][NP - 1 :] + terms[r + 1][:1] for r in range(RAD - 1)] + [zero]
            for r in range(RAD):
                whole = jnp.concatenate([joins[r], terms[r][1 : NP - 1], joins[r + 1]], axis=0)
                p = r * AZ + outer
                bf[c, p, edge_o, :] = bf[c, p, edge_o, :] + whole

    def inner_joints(c):
        for r in range(RAD):
            for outer, edge_o, inner, edge_i in seams:
                bf[c, r * AZ + inner, edge_i, :] = bf[c, r * AZ + outer, edge_o, :]
            p = r * AZ + 1
            shared = bf[c, p, last_edge, :] + bf[c, p + 1, first_edge, :]
            bf[c, p, last_edge, :] = shared
            bf[c, p + 1, first_edge, :] = shared

    for c in range(2):
        outer_seams(c)
    for c in range(2):
        rims_finish(bf, c, 0, b_flights[c])
        apply(c, outside)
        radial(yf, c, outside)
        y_flights.append(rims_start(yf, c, 1))
    for c in range(2):
        wait_returns(1, c)
        rhs(c, inside)
        inner_joints(c)
        apply(c, inside)
        radial(yf, c, inside)
        joints(yf, c)
        energy(c, inside)
    for c in range(2):
        rims_finish(yf, c, 1, y_flights[c])
        energy(c, outside)

    sums = jnp.concatenate(
        [jnp.sum(acc[c, k], axis=0, keepdims=True) for c in range(2) for k in range(4)], axis=0
    )

    part[...] = sums
    if y_peers:
        pl.semaphore_wait(known, len(y_peers))
    for k, peer in enumerate(all_peers):
        copy = pltpu.make_async_remote_copy(
            src_ref=part,
            dst_ref=gat.at[me_e],
            send_sem=as_all.at[k],
            recv_sem=ar_all.at[me_e],
            device_id=(peer, me),
            device_id_type=MESH,
        )
        copy.start()
        halo_sends.append(copy)
    gat[me_e] = sums
    for k, peer in enumerate(all_peers):
        pltpu.make_async_remote_copy(
            src_ref=part,
            dst_ref=gat.at[peer],
            send_sem=as_all.at[k],
            recv_sem=ar_all.at[peer],
            device_id=(peer, me),
            device_id_type=MESH,
        ).wait_recv()
    sums = jnp.sum(gat[...], axis=0)

    for c in range(2):
        m0, m1, m2, m3 = (sums[c * 4 + k : c * 4 + k + 1] for k in range(4))
        alpha = m0 / m1
        grown = alpha * alpha * m2 - m0
        scale = 1.0 + grown / m0
        below = scale * scale * m1 - 2.0 * scale * alpha * m2 + alpha * alpha * m3
        beyond = grown / below
        on_b = alpha + beyond * scale
        on_y = -beyond * alpha

        def combine(s, carry, c=c, on_b=on_b, on_y=on_y):
            p = inverse[s]
            grid = on_b * bf[c, p] + on_y * yf[c, p]
            outs[c][pl.ds(s, NODES, stride=ELEMS), :] = grid[:NODES]
            return carry

        lax.fori_loop(0, ELEMS, combine, 0, unroll=4)

    for copy in sends + ret_sends + halo_sends:
        copy.wait_send()


def body(size_e, vel_x, vel_y, metrics, slot_order):
    there, back, gmat, dmat = constants()
    any_space = pl.BlockSpec(memory_space=pl.ANY)
    vmem = pl.BlockSpec(memory_space=pltpu.VMEM)
    smem = pl.BlockSpec(memory_space=pltpu.SMEM)
    dma = pltpu.SemaphoreType.DMA
    rows = NODES * ELEMS
    out_x, out_y = pl.pallas_call(
        functools.partial(kernel, size_e),
        out_shape=[pltpu.VMEM((rows, LANES), F32)] * 2,
        in_specs=[any_space] * 3 + [smem] + [any_space] * 4,
        out_specs=[vmem, vmem],
        scratch_shapes=[
            pltpu.VMEM((2, rows, LANES), F32),
            pltpu.VMEM((8, ELEMS, NODES), F32),
            pltpu.VMEM(there.shape, BF16),
            pltpu.VMEM(back.shape, BF16),
            pltpu.VMEM(gmat.shape, BF16),
            pltpu.VMEM(dmat.shape, BF16),
            pltpu.VMEM((ELEMS, 2, ROWS, LANES), F32),
            pltpu.VMEM((GROUPS, 2, 2, ROWS, LANES), F32),
            pltpu.VMEM((4 * ROWS, MODES), BF16),
            pltpu.VMEM((4 * KROWS, PLANES), BF16),
            pltpu.VMEM((2, 4, ROWS, LANES), F32),
            pltpu.VMEM((4, ELEMS, ROWS, LANES), F32),
            pltpu.VMEM((RAD, ROWS, LANES), F32),
            pltpu.VMEM((2, GROUPS, 2, ROWS, LANES), F32),
            pltpu.VMEM((ELEMS, 2, ROWS, LANES), F32),
            pltpu.VMEM((2, ELEMS, ROWS, LANES), F32),
            pltpu.VMEM((2, ELEMS, ROWS, LANES), F32),
            pltpu.VMEM((2, 2, 2, RAD, 16, LANES), F32),
            pltpu.VMEM((2, 2, 2, RAD, 16, LANES), F32),
            pltpu.VMEM((2, 4, 8, LANES), F32),
            pltpu.VMEM((8, LANES), F32),
            pltpu.VMEM((size_e, 8, LANES), F32),
            dma((7,)),
            dma((2, GROUPS)),
            dma((2, GROUPS)),
            dma((6,)),
            dma((2, 2, GROUPS)),
            dma((2, 2, GROUPS)),
            dma((2, 2, 2)),
            dma((2, 2, 2)),
            dma((size_e,)),
            dma((size_e,)),
            pltpu.SemaphoreType.REGULAR,
            pltpu.SMEM((ELEMS,), jnp.int32),
            pltpu.VMEM((GROUPS, 2, 16, LANES), F32),
            pltpu.VMEM((GROUPS, 2, 16, LANES), F32),
            dma((GROUPS,)),
            dma((GROUPS,)),
        ],
        compiler_params=pltpu.CompilerParams(
            collective_id=0, has_side_effects=True, vmem_limit_bytes=56 * 2**20
        ),
    )(
        vel_x.reshape(rows, LANES),
        vel_y.reshape(rows, LANES),
        metrics.transpose(0, 2, 1),
        slot_order,
        jnp.asarray(there),
        jnp.asarray(back),
        jnp.asarray(gmat),
        jnp.asarray(dmat),
    )
    shape = (NODES, ELEMS, LANES)
    return out_x.reshape(shape), out_y.reshape(shape)


def solution(mesh):
    placed = (P(None, "elem", "mode"), P(None, "elem", "mode"), P(None, None, "elem"), P("elem"))
    return jax.shard_map(
        functools.partial(body, mesh.shape["elem"]),
        mesh=mesh,
        in_specs=placed,
        out_specs=(P(None, "elem", "mode"), P(None, "elem", "mode")),
        check_vma=False,
    )
```

```python
import functools
import math

import jax
import jax.numpy as jnp
import ml_dtypes
import numpy as np
from jax import lax
from jax.experimental import pallas as pl
from jax.experimental.pallas import tpu as pltpu
from jax.sharding import PartitionSpec as P

ORDER = 8
NP = ORDER + 1
NODES = NP * NP
ROWS = 88
KROWS = 96
EDGE = NODES - NP
RAD = 4
AZ = 4
ELEMS = 16
MODES = 1024
PLANES = 1536
LANES = 128
CHUNK = 256
GROUPS = 8
ZRING = 8
SIGMA = 2.0
WAVE = 64.0
PIECES = 2
MESH = pl.DeviceIdType.MESH
F32 = jnp.float32
BF16 = jnp.bfloat16


def legendre_value(order, point):
    previous = 1.0
    current = point
    for degree in range(2, order + 1):
        previous, current = (
            current,
            ((2 * degree - 1) * point * current - (degree - 1) * previous) / degree,
        )
    return (current, previous)


def gll_matrix(order):
    points = []
    for index in range(order + 1):
        point = -math.cos(math.pi * index / order)
        for sweep in range(100):
            high, lower = legendre_value(order, point)
            point = point - (point * high - lower) / ((order + 1) * high)
        points.append(point)
    points[0] = -1.0
    points[order] = 1.0
    values = [legendre_value(order, point)[0] for point in points]
    number = order + 1
    matrix = np.zeros((number, number))
    for row_index in range(number):
        for col_index in range(number):
            if row_index != col_index:
                matrix[row_index, col_index] = values[row_index] / (
                    values[col_index] * (points[row_index] - points[col_index])
                )
    matrix[0, 0] = -order * (order + 1) / 4.0
    matrix[order, order] = order * (order + 1) / 4.0
    return matrix


def halves(array):
    array = np.asarray(array, np.float32)
    high = array.astype(ml_dtypes.bfloat16)
    low = (array - high.astype(np.float32)).astype(ml_dtypes.bfloat16)
    return high, low


@functools.lru_cache(maxsize=None)
def constants():
    wave = np.arange(MODES)
    freq = (wave + 1) // 2
    phase = freq[:, None] * np.arange(PLANES)[None, :] % PLANES
    angle = 2.0 * np.pi / PLANES * phase
    table = np.where((wave % 2 == 0)[:, None], np.cos(angle), np.sin(angle))
    table = table * np.where(wave == 0, math.sqrt(1.0 / PLANES), math.sqrt(2.0 / PLANES))[:, None]
    high, low = halves(table)
    there = np.stack([high, low]).reshape(2, MODES, PLANES // CHUNK, CHUNK).transpose(0, 2, 1, 3)
    back = np.stack([high.T, low.T]).reshape(2, PLANES, MODES // CHUNK, CHUNK).transpose(0, 2, 1, 3)
    dmat = gll_matrix(ORDER).astype(np.float32)
    eye = np.eye(NP, dtype=np.float32)
    grad = np.zeros((2, ROWS, ROWS), np.float32)
    grad[0, :NODES, :NODES] = np.kron(dmat, eye)
    grad[1, :NODES, :NODES] = np.kron(eye, dmat)
    ghigh, glow = halves(grad.reshape(2 * ROWS, ROWS))
    gmat = np.zeros((4 * ROWS, 2 * KROWS), ml_dtypes.bfloat16)
    gmat[: 2 * ROWS, :ROWS] = ghigh
    gmat[: 2 * ROWS, KROWS : KROWS + ROWS] = ghigh
    gmat[2 * ROWS :, :ROWS] = glow
    dhigh, dlow = halves(grad.transpose(2, 0, 1).reshape(ROWS, 2 * ROWS))
    dmat2 = np.zeros((2 * KROWS, 2 * ROWS), ml_dtypes.bfloat16)
    dmat2[:ROWS] = dhigh
    dmat2[KROWS : KROWS + ROWS] = dlow
    return np.ascontiguousarray(there), np.ascontiguousarray(back), gmat, dmat2


def split(value):
    high = value.astype(BF16)
    return high, (value - high.astype(F32)).astype(BF16)


def split_rows(value):
    high = value.astype(BF16).astype(F32)
    gap = jnp.zeros((KROWS - ROWS, value.shape[1]), F32)
    return jnp.concatenate([high, gap, value - high, gap], axis=0).astype(BF16)


def mm(a, b):
    return jnp.dot(a, b, preferred_element_type=F32)


def fold(value):
    total = jnp.sum(value.reshape(ROWS // 8, 8, value.shape[1]), axis=0)
    out = total[:, :LANES]
    for at in range(1, value.shape[1] // LANES):
        out = out + total[:, at * LANES : (at + 1) * LANES]
    return out


def position(rank, second):
    row, side = rank // 2, rank % 2
    return row * AZ + (1 + side if second else (AZ - 1) * side)


def kernel(
    size_e,
    velx_hbm,
    vely_hbm,
    met_hbm,
    slots,
    there_hbm,
    back_hbm,
    gmat_hbm,
    dmat_hbm,
    b_x,
    b_y,
    y_x,
    y_y,
    coef,
    vel,
    met,
    there,
    back,
    gmat,
    dmat,
    snd,
    rv,
    act,
    wave,
    pgeo,
    geo,
    wts,
    ret,
    rv2,
    pack,
    bf,
    yf,
    hs,
    hr,
    acc,
    part,
    gat,
    in_sem,
    s1,
    r1,
    own,
    s2,
    r2,
    hsem,
    hrem,
    as_all,
    ar_all,
    known,
    inverse,
    esnd,
    ercv,
    es,
    er,
):
    outs_b, outs_y = (b_x, b_y), (y_x, y_y)
    me_e = lax.axis_index("elem")
    me = lax.axis_index("mode")
    chip, core = me // 2, me % 2
    zed, why = me_e % ZRING, me_e // ZRING
    size_y = size_e // ZRING
    left = (me_e + size_e - 1) % size_e
    right = (me_e + 1) % size_e
    peers = [
        (((chip + dc) % 4) * 2 + (core + cc) % 2)
        for dc, cc in ((2, 0), (2, 1), (1, 0), (3, 0), (1, 1), (3, 1), (0, 1))
    ]
    z_peers = [why * ZRING + (zed + k) % ZRING for k in (4, 3, 5, 2, 6, 1, 7)]
    y_peers = [((why + k) % size_y) * ZRING + zed for k in range(1, size_y)]

    def hops(step):
        return min(step[0], size_y - step[0]) + min(step[1], ZRING - step[1])

    steps = [(dy, dz) for dy in range(size_y) for dz in range(ZRING) if dy or dz]
    all_peers = [
        ((why + dy) % size_y) * ZRING + (zed + dz) % ZRING
        for dy, dz in sorted(steps, key=lambda step: -hops(step))
    ]

    loads = [
        pltpu.make_async_copy(velx_hbm, vel.at[0], in_sem.at[0]),
        pltpu.make_async_copy(vely_hbm, vel.at[1], in_sem.at[1]),
        pltpu.make_async_copy(met_hbm, met, in_sem.at[2]),
        pltpu.make_async_copy(gmat_hbm, gmat, in_sem.at[3]),
        pltpu.make_async_copy(dmat_hbm, dmat, in_sem.at[4]),
        pltpu.make_async_copy(there_hbm, there, in_sem.at[5]),
        pltpu.make_async_copy(back_hbm, back, in_sem.at[6]),
    ]
    for copy in loads[:5]:
        copy.start()

    tail = jnp.zeros((2, 8, LANES), F32)
    for p in range(ELEMS):
        snd[p, :, ROWS - 8 :, :] = tail
        rv[p // 2, p % 2, :, ROWS - 8 :, :] = tail

    barrier = pltpu.get_barrier_semaphore()
    for peer in peers:
        pl.semaphore_signal(barrier, inc=1, device_id=(me_e, peer), device_id_type=MESH)
    for peer in z_peers + y_peers + [left, right]:
        pl.semaphore_signal(barrier, inc=1, device_id=(peer, me), device_id_type=MESH)

    pl.semaphore_wait(barrier, len(peers) + len(z_peers) + len(y_peers) + 2)

    for peer in y_peers:
        pl.semaphore_signal(known, inc=1, device_id=(peer, me), device_id_type=MESH)

    loads[0].wait()
    loads[1].wait()

    def gather(p):
        slot = slots[p]
        for c in range(2):
            snd[p, c, 0:NODES, :] = vel[c, pl.ds(slot, NODES, stride=ELEMS), :]

    sends = []
    arrivals = [[], []]
    locals_ = []
    for e in range(2):
        for k, peer in enumerate(peers):
            p = position(peer, e)
            gather(p)
            copy = pltpu.make_async_remote_copy(
                src_ref=snd.at[p, :, pl.ds(0, NODES)],
                dst_ref=rv.at[me, e, :, pl.ds(0, NODES)],
                send_sem=s1.at[e, k],
                recv_sem=r1.at[e, me],
                device_id=(me_e, peer),
                device_id_type=MESH,
            )
            copy.start()
            sends.append(copy)
        p = position(me, e)
        gather(p)
        copy = pltpu.make_async_copy(
            snd.at[p, :, pl.ds(0, NODES)], rv.at[me, e, :, pl.ds(0, NODES)], own.at[e]
        )
        copy.start()
        locals_.append(copy)
        for k, peer in enumerate(peers):
            arrivals[e].append(
                pltpu.make_async_remote_copy(
                    src_ref=snd.at[0, :, pl.ds(0, NODES)],
                    dst_ref=rv.at[peer, e, :, pl.ds(0, NODES)],
                    send_sem=s1.at[e, k],
                    recv_sem=r1.at[e, peer],
                    device_id=(me_e, peer),
                    device_id_type=MESH,
                )
            )

    loads[5].start()
    loads[6].start()

    loads[2].wait()
    loads[3].wait()
    loads[4].wait()
    row16 = lax.broadcasted_iota(jnp.int32, (ELEMS, LANES), 0)

    def picker(p):
        return jnp.where(row16 == slots[p], 1.0, 0.0).astype(BF16)

    def spread(factors, pick):
        gap = jnp.zeros((ELEMS, ROWS - NODES), F32)
        full = jnp.concatenate([factors, gap], axis=1).T
        high = full.astype(BF16)
        rest = full - high.astype(F32)
        mid = rest.astype(BF16)
        low = (rest - mid.astype(F32)).astype(BF16)
        return mm(high, pick) + mm(mid, pick) + mm(low, pick)

    mine = jnp.concatenate([picker(position(me, 0)), picker(position(me, 1))], axis=1)
    jac = spread(met[7], mine)
    for g in range(4):
        full = spread(met[g], mine) * jac
        pgeo[0, g] = full[:, :LANES]
        pgeo[1, g] = full[:, LANES:]

    def spread_row(r, carry):
        pick = jnp.concatenate([picker(r * AZ + a) for a in range(AZ)], axis=1)
        for g in range(4):
            full = spread(met[4 + g], pick)
            for a in range(AZ):
                geo[g, r * AZ + a] = full[:, a * LANES : (a + 1) * LANES]
        return carry

    lax.fori_loop(0, RAD, spread_row, 0)

    node = lax.broadcasted_iota(jnp.int32, (ROWS, LANES), 0)
    along = node % NP
    sides = jnp.where((along == 0) | (along == NP - 1), 0.5, 1.0).astype(F32)
    sides = jnp.where(node < NODES, sides, 0.0)
    first, last = node < NP, node >= EDGE
    wts[0] = jnp.where(first, 0.0, jnp.where(last, 0.5, 1.0)) * sides
    wts[1] = jnp.where(first | last, 0.5, 1.0) * sides
    wts[2] = wts[1]
    wts[3] = jnp.where(last, 0.0, jnp.where(first, 0.5, 1.0)) * sides

    lane = lax.broadcasted_iota(jnp.int32, (1, LANES), 1) + me * LANES
    freq = ((lane + 1) // 2).astype(F32) / WAVE
    lam = SIGMA + freq * freq

    acc[...] = jnp.zeros_like(acc)

    stored = [slots[p] for p in range(ELEMS)]
    for s in range(ELEMS):
        place = jnp.int32(0)
        for p in range(1, ELEMS):
            place = jnp.where(stored[p] == s, jnp.int32(p), place)
        inverse[s] = place

    def prior(p, carry):
        twice = SIGMA * geo[3, p]
        for c in range(2):
            bf[c, p] = twice * snd[p, c]
        return carry

    lax.fori_loop(0, ELEMS, prior, 0)

    ret_sends = []
    ret_locals = [[], []]

    side = me % 2

    def send_back(e, c):
        start = 1 - side if e else side

        def pack_rank(rank, carry):
            for i in range(NP):
                pack[e, rank, c, 8 * i : 8 * i + 8] = ret[e, rank, c, pl.ds(NP * i + start, 8), :]
            return carry

        lax.fori_loop(0, GROUPS, pack_rank, 0, unroll=2)
        for k, peer in enumerate(peers):
            copy = pltpu.make_async_remote_copy(
                src_ref=pack.at[e, peer, c],
                dst_ref=rv2.at[position(me, e), c],
                send_sem=s2.at[e, c, k],
                recv_sem=r2.at[e, c, me],
                device_id=(me_e, peer),
                device_id_type=MESH,
            )
            copy.start()
            ret_sends.append(copy)
        copy = pltpu.make_async_copy(
            pack.at[e, me, c],
            rv2.at[position(me, e), c],
            own.at[2 + 2 * e + c],
        )
        copy.start()
        ret_locals[c].append(copy)
    for e in range(2):
        for copy in arrivals[e]:
            copy.wait_recv()
        locals_[e].wait()
        for src in range(GROUPS):
            both = rv[src, e].reshape(2 * ROWS, LANES)
            high, low = split(both)
            act[0 : 2 * ROWS, src * LANES : (src + 1) * LANES] = high
            act[2 * ROWS :, src * LANES : (src + 1) * LANES] = low
        if e == 0:
            loads[5].wait()

        def planes(z, carry, e=e):
            top = mm(act[...], there[0, z])
            field = top[: 2 * ROWS] + top[2 * ROWS :] + mm(act[0 : 2 * ROWS, :], there[1, z])
            u, v = field[:ROWS], field[ROWS:]
            diff = mm(gmat[...], split_rows(jnp.concatenate([u, v], axis=1)))
            diff = diff[: 2 * ROWS] + diff[2 * ROWS :]
            m = [jnp.concatenate([pgeo[e, g]] * (CHUNK // LANES), axis=1) for g in range(4)]
            by_i = u * m[0] + v * m[2]
            by_j = u * m[1] + v * m[3]
            for c in range(2):
                cols = slice(c * CHUNK, (c + 1) * CHUNK)
                prod = by_i * diff[:ROWS, cols] + by_j * diff[ROWS:, cols]
                at = pl.ds(pl.multiple_of(z * CHUNK, CHUNK), CHUNK)
                wave[c * 2 * KROWS : (c + 1) * 2 * KROWS, at] = split_rows(prod)
            return carry

        lax.fori_loop(0, PLANES // CHUNK, planes, 0, unroll=3)
        if e == 0:
            loads[6].wait()

        for c in range(2):
            for step, dc in enumerate((2, 1, 3, 0)):
                n = (chip + dc) % 4
                top = mm(wave[c * 2 * KROWS : (c + 1) * 2 * KROWS, :], back[0, n])
                low = mm(wave[c * 2 * KROWS : c * 2 * KROWS + KROWS, :], back[1, n])
                hat = top[:ROWS] + top[KROWS : KROWS + ROWS] + low[:ROWS]
                for half in range(2):
                    ret[e, n * 2 + half, c] = hat[:, half * LANES : (half + 1) * LANES]
            if e == 0:
                send_back(e, c)
        if e == 1:
            near = pl.ds(side * (NP - 1), NP, stride=NP)
            far = pl.ds((1 - side) * (NP - 1), NP, stride=NP)
            for rank in range(GROUPS):
                for c in range(2):
                    esnd[rank, c, 0:NP] = ret[1, rank, c, near, :] + ret[0, rank, c, far, :]
            for k, peer in enumerate(peers):
                copy = pltpu.make_async_remote_copy(
                    src_ref=esnd.at[peer, :, pl.ds(0, NP)],
                    dst_ref=ercv.at[me, :, pl.ds(0, NP)],
                    send_sem=es.at[k],
                    recv_sem=er.at[me],
                    device_id=(me_e, peer),
                    device_id_type=MESH,
                )
                copy.start()
                ret_sends.append(copy)
            for c in range(2):
                ercv[me, c, 0:NP] = esnd[me, c, 0:NP]
                send_back(e, c)

    def wait_returns(e, c):
        for peer in peers:
            pltpu.make_async_remote_copy(
                src_ref=pack.at[e, 0, c],
                dst_ref=rv2.at[position(peer, e), c],
                send_sem=s2.at[e, c, 0],
                recv_sem=r2.at[e, c, peer],
                device_id=(me_e, peer),
                device_id_type=MESH,
            ).wait_recv()
        ret_locals[c][e].wait()

    halo_sends = []

    def radial(field, c, cols):
        for a in cols:
            for r in range(RAD - 1):
                up, down = r * AZ + a, (r + 1) * AZ + a
                joined = field[c, up, EDGE : EDGE + 8] + field[c, down, 0:8]
                corner = field[c, up, EDGE + 8 : NODES] + field[c, down, 8:NP]
                field[c, up, EDGE : EDGE + 8] = joined
                field[c, down, 0:8] = joined
                field[c, up, EDGE + 8 : NODES] = corner
                field[c, down, 8:NP] = corner
            field[c, a, 0:8] = jnp.zeros((8, LANES), F32)
            field[c, a, 8:NP] = jnp.zeros((1, LANES), F32)
            end = (RAD - 1) * AZ + a
            field[c, end, EDGE : EDGE + 8] = jnp.zeros((8, LANES), F32)
            field[c, end, EDGE + 8 : NODES] = jnp.zeros((1, LANES), F32)

    first_edge = pl.ds(0, NP, stride=NP)
    last_edge = pl.ds(NP - 1, NP, stride=NP)

    def rims_start(field, c, which):
        for r in range(RAD):
            hs[which, c, 0, r, 0:NP] = field[c, r * AZ, first_edge, :]
            hs[which, c, 1, r, 0:NP] = field[c, r * AZ + AZ - 1, last_edge, :]
        copies = []
        for side, peer in ((0, left), (1, right)):
            copy = pltpu.make_async_remote_copy(
                src_ref=hs.at[which, c, side, :, pl.ds(0, NP)],
                dst_ref=hr.at[which, c, side, :, pl.ds(0, NP)],
                send_sem=hsem.at[which, c, side],
                recv_sem=hrem.at[which, c, side],
                device_id=(peer, me),
                device_id_type=MESH,
            )
            copy.start()
            copies.append(copy)
        halo_sends.extend(copies)
        return copies

    def joints(field, c):
        for r in range(RAD):
            for a in range(AZ - 1):
                p = r * AZ + a
                shared = field[c, p, last_edge, :] + field[c, p + 1, first_edge, :]
                field[c, p, last_edge, :] = shared
                field[c, p + 1, first_edge, :] = shared

    def rims_finish(field, c, which, copies):
        for copy in copies:
            copy.wait_recv()
        for r in range(RAD):
            p = r * AZ + AZ - 1
            field[c, p, last_edge, :] = field[c, p, last_edge, :] + hr[which, c, 0, r, 0:NP]
            p = r * AZ
            field[c, p, first_edge, :] = field[c, p, first_edge, :] + hr[which, c, 1, r, 0:NP]

    def pair(ref, c, p0, p1):
        return jnp.concatenate([ref[c, p0], ref[c, p1]], axis=1)

    def fluxes(x, p0, p1):
        diff = mm(gmat[...], split_rows(x))
        diff = diff[: 2 * ROWS] + diff[2 * ROWS :]
        x_i, x_j = diff[:ROWS], diff[ROWS:]
        g = [pair(geo, k, p0, p1) for k in range(4)]
        return x_i, x_j, g[0] * x_i + g[1] * x_j, g[1] * x_i + g[2] * x_j, g[3]

    lam2 = jnp.concatenate([lam, lam], axis=1)

    def weights(r):
        return jnp.concatenate([wts[r], wts[r]], axis=1)

    def apply(c, cols):
        def step(r, carry):
            p0, p1 = r * AZ + cols[0], r * AZ + cols[1]
            x = pair(bf, c, p0, p1)
            x_i, x_j, f_i, f_j, jw = fluxes(x, p0, p1)
            high, low = split(jnp.concatenate([f_i, f_j], axis=0))
            top = mm(dmat[...], high)
            y = top[:ROWS] + top[KROWS : KROWS + ROWS] + mm(dmat[0:KROWS, :], low)[:ROWS]
            y = y + lam2 * jw * x
            yf[c, p0] = y[:, :LANES]
            yf[c, p1] = y[:, LANES:]
            acc[c, 0] = acc[c, 0] + fold(x * x * weights(r))
            acc[c, 1] = acc[c, 1] + fold(x * y)
            return carry

        lax.fori_loop(0, RAD, step, 0, unroll=4)

    def energy(c, cols):
        def step(r, carry):
            p0, p1 = r * AZ + cols[0], r * AZ + cols[1]
            y = pair(yf, c, p0, p1)
            y_i, y_j, f_i, f_j, jw = fluxes(y, p0, p1)
            acc[c, 2] = acc[c, 2] + fold(y * y * weights(r))
            acc[c, 3] = acc[c, 3] + fold(f_i * y_i + f_j * y_j + lam2 * jw * y * y)
            return carry

        lax.fori_loop(0, RAD, step, 0, unroll=4)

    def rhs(c, cols):
        for r in range(RAD):
            for a in cols:
                p = r * AZ + a
                for i in range(NP):
                    at = slice(NP * i + a % 2, NP * i + a % 2 + 8)
                    bf[c, p, at] = bf[c, p, at] - rv2[p, c, 8 * i : 8 * i + 8]
        radial(bf, c, cols)

    inside, outside = (1, 2), (0, AZ - 1)
    b_flights, y_flights = [], []
    for c in range(2):
        wait_returns(0, c)
        rhs(c, outside)
        b_flights.append(rims_start(bf, c, 0))
    for peer in peers:
        pltpu.make_async_remote_copy(
            src_ref=esnd.at[peer, :, pl.ds(0, NP)],
            dst_ref=ercv.at[peer, :, pl.ds(0, NP)],
            send_sem=es.at[0],
            recv_sem=er.at[peer],
            device_id=(me_e, peer),
            device_id_type=MESH,
        ).wait_recv()

    seams = ((0, last_edge, 1, first_edge), (AZ - 1, first_edge, AZ - 2, last_edge))

    def outer_seams(c):
        for side, (outer, edge_o, inner, edge_i) in enumerate(seams):
            terms = [
                bf[c, r * AZ + inner, edge_i, :] - ercv[2 * r + side, c, 0:NP] for r in range(RAD)
            ]
            zero = jnp.zeros((1, LANES), F32)
            joins = [zero] + [terms[r][NP - 1 :] + terms[r + 1][:1] for r in range(RAD - 1)] + [zero]
            for r in range(RAD):
                whole = jnp.concatenate([joins[r], terms[r][1 : NP - 1], joins[r + 1]], axis=0)
                p = r * AZ + outer
                bf[c, p, edge_o, :] = bf[c, p, edge_o, :] + whole

    def inner_joints(c):
        for r in range(RAD):
            for outer, edge_o, inner, edge_i in seams:
                bf[c, r * AZ + inner, edge_i, :] = bf[c, r * AZ + outer, edge_o, :]
            p = r * AZ + 1
            shared = bf[c, p, last_edge, :] + bf[c, p + 1, first_edge, :]
            bf[c, p, last_edge, :] = shared
            bf[c, p + 1, first_edge, :] = shared

    for c in range(2):
        outer_seams(c)
    for c in range(2):
        rims_finish(bf, c, 0, b_flights[c])
        apply(c, outside)
        radial(yf, c, outside)
        y_flights.append(rims_start(yf, c, 1))
    for c in range(2):
        wait_returns(1, c)
        rhs(c, inside)
        inner_joints(c)
        apply(c, inside)
        radial(yf, c, inside)
        joints(yf, c)
        energy(c, inside)
    for c in range(2):
        rims_finish(yf, c, 1, y_flights[c])
        energy(c, outside)

    sums = jnp.concatenate(
        [jnp.sum(acc[c, k], axis=0, keepdims=True) for c in range(2) for k in range(4)], axis=0
    )

    part[...] = sums
    if y_peers:
        pl.semaphore_wait(known, len(y_peers))
    for k, peer in enumerate(all_peers):
        copy = pltpu.make_async_remote_copy(
            src_ref=part,
            dst_ref=gat.at[me_e],
            send_sem=as_all.at[k],
            recv_sem=ar_all.at[me_e],
            device_id=(peer, me),
            device_id_type=MESH,
        )
        copy.start()
        halo_sends.append(copy)
    gat[me_e] = sums
    for c in range(2):

        def store(s, carry, c=c):
            p = inverse[s]
            at = pl.ds(s, NODES, stride=ELEMS)
            outs_b[c][at, :] = bf[c, p, 0:NODES]
            outs_y[c][at, :] = yf[c, p, 0:NODES]
            return carry

        lax.fori_loop(0, ELEMS, store, 0, unroll=4)
    for k, peer in enumerate(all_peers):
        pltpu.make_async_remote_copy(
            src_ref=part,
            dst_ref=gat.at[peer],
            send_sem=as_all.at[k],
            recv_sem=ar_all.at[peer],
            device_id=(peer, me),
            device_id_type=MESH,
        ).wait_recv()
    sums = jnp.sum(gat[...], axis=0)

    for c in range(2):
        m0, m1, m2, m3 = (sums[c * 4 + k : c * 4 + k + 1] for k in range(4))
        alpha = m0 / m1
        grown = alpha * alpha * m2 - m0
        scale = 1.0 + grown / m0
        below = scale * scale * m1 - 2.0 * scale * alpha * m2 + alpha * alpha * m3
        beyond = grown / below
        on_b = alpha + beyond * scale
        on_y = -beyond * alpha

        coef[2 * c : 2 * c + 1] = on_b
        coef[2 * c + 1 : 2 * c + 2] = on_y

    for copy in sends + ret_sends + halo_sends:
        copy.wait_send()


def combine_kernel(b_x, b_y, y_x, y_y, coef, out_x, out_y, held, sem):
    size = b_x.shape[0] // PIECES
    copies = []
    for piece in range(PIECES):
        at = pl.ds(piece * size, size)
        for c, (b, y, out) in enumerate(((b_x, y_x, out_x), (b_y, y_y, out_y))):
            held[c, at] = coef[2 * c : 2 * c + 1] * b[at] + coef[2 * c + 1 : 2 * c + 2] * y[at]
            copy = pltpu.make_async_copy(held.at[c, at], out.at[at], sem.at[c, piece])
            copy.start()
            copies.append(copy)
    for copy in copies:
        copy.wait()


def body(size_e, vel_x, vel_y, metrics, slot_order):
    there, back, gmat, dmat = constants()
    any_space = pl.BlockSpec(memory_space=pl.ANY)
    vmem = pl.BlockSpec(memory_space=pltpu.VMEM)
    smem = pl.BlockSpec(memory_space=pltpu.SMEM)
    dma = pltpu.SemaphoreType.DMA
    rows = NODES * ELEMS
    b_x, b_y, y_x, y_y, coef = pl.pallas_call(
        functools.partial(kernel, size_e),
        out_shape=[pltpu.VMEM((rows, LANES), F32)] * 4 + [pltpu.VMEM((8, LANES), F32)],
        in_specs=[any_space] * 3 + [smem] + [any_space] * 4,
        out_specs=[vmem] * 5,
        scratch_shapes=[
            pltpu.VMEM((2, rows, LANES), F32),
            pltpu.VMEM((8, ELEMS, NODES), F32),
            pltpu.VMEM(there.shape, BF16),
            pltpu.VMEM(back.shape, BF16),
            pltpu.VMEM(gmat.shape, BF16),
            pltpu.VMEM(dmat.shape, BF16),
            pltpu.VMEM((ELEMS, 2, ROWS, LANES), F32),
            pltpu.VMEM((GROUPS, 2, 2, ROWS, LANES), F32),
            pltpu.VMEM((4 * ROWS, MODES), BF16),
            pltpu.VMEM((4 * KROWS, PLANES), BF16),
            pltpu.VMEM((2, 4, ROWS, LANES), F32),
            pltpu.VMEM((4, ELEMS, ROWS, LANES), F32),
            pltpu.VMEM((RAD, ROWS, LANES), F32),
            pltpu.VMEM((2, GROUPS, 2, ROWS, LANES), F32),
            pltpu.VMEM((ELEMS, 2, NP * ORDER, LANES), F32),
            pltpu.VMEM((2, GROUPS, 2, NP * ORDER, LANES), F32),
            pltpu.VMEM((2, ELEMS, ROWS, LANES), F32),
            pltpu.VMEM((2, ELEMS, ROWS, LANES), F32),
            pltpu.VMEM((2, 2, 2, RAD, 16, LANES), F32),
            pltpu.VMEM((2, 2, 2, RAD, 16, LANES), F32),
            pltpu.VMEM((2, 4, 8, LANES), F32),
            pltpu.VMEM((8, LANES), F32),
            pltpu.VMEM((size_e, 8, LANES), F32),
            dma((7,)),
            dma((2, GROUPS)),
            dma((2, GROUPS)),
            dma((6,)),
            dma((2, 2, GROUPS)),
            dma((2, 2, GROUPS)),
            dma((2, 2, 2)),
            dma((2, 2, 2)),
            dma((size_e,)),
            dma((size_e,)),
            pltpu.SemaphoreType.REGULAR,
            pltpu.SMEM((ELEMS,), jnp.int32),
            pltpu.VMEM((GROUPS, 2, 16, LANES), F32),
            pltpu.VMEM((GROUPS, 2, 16, LANES), F32),
            dma((GROUPS,)),
            dma((GROUPS,)),
        ],
        compiler_params=pltpu.CompilerParams(
            collective_id=0, has_side_effects=True, vmem_limit_bytes=56 * 2**20
        ),
    )(
        vel_x.reshape(rows, LANES),
        vel_y.reshape(rows, LANES),
        metrics.transpose(0, 2, 1),
        slot_order,
        jnp.asarray(there),
        jnp.asarray(back),
        jnp.asarray(gmat),
        jnp.asarray(dmat),
    )
    out_x, out_y = pl.pallas_call(
        combine_kernel,
        out_shape=[jax.ShapeDtypeStruct((rows, LANES), F32)] * 2,
        in_specs=[vmem] * 5,
        out_specs=[any_space] * 2,
        scratch_shapes=[pltpu.VMEM((2, rows, LANES), F32), dma((2, PIECES))],
        compiler_params=pltpu.CompilerParams(vmem_limit_bytes=16 * 2**20),
    )(b_x, b_y, y_x, y_y, coef)
    shape = (NODES, ELEMS, LANES)
    return out_x.reshape(shape), out_y.reshape(shape)


def solution(mesh):
    placed = (P(None, "elem", "mode"), P(None, "elem", "mode"), P(None, None, "elem"), P("elem"))
    return jax.shard_map(
        functools.partial(body, mesh.shape["elem"]),
        mesh=mesh,
        in_specs=placed,
        out_specs=(P(None, "elem", "mode"), P(None, "elem", "mode")),
        check_vma=False,
    )
```

```python
import functools
import math

import jax
import jax.numpy as jnp
import ml_dtypes
import numpy as np
from jax import lax
from jax.experimental import pallas as pl
from jax.experimental.pallas import tpu as pltpu
from jax.sharding import PartitionSpec as P

ORDER = 8
NP = ORDER + 1
NODES = NP * NP
ROWS = 88
KROWS = 96
EDGE = NODES - NP
RAD = 4
AZ = 4
ELEMS = 16
MODES = 1024
PLANES = 1536
LANES = 128
CHUNK = 256
GROUPS = 8
ZRING = 8
SIGMA = 2.0
WAVE = 64.0
PIECES = 2
MESH = pl.DeviceIdType.MESH
F32 = jnp.float32
BF16 = jnp.bfloat16


def legendre_value(order, point):
    previous = 1.0
    current = point
    for degree in range(2, order + 1):
        previous, current = (
            current,
            ((2 * degree - 1) * point * current - (degree - 1) * previous) / degree,
        )
    return (current, previous)


def gll_matrix(order):
    points = []
    for index in range(order + 1):
        point = -math.cos(math.pi * index / order)
        for sweep in range(100):
            high, lower = legendre_value(order, point)
            point = point - (point * high - lower) / ((order + 1) * high)
        points.append(point)
    points[0] = -1.0
    points[order] = 1.0
    values = [legendre_value(order, point)[0] for point in points]
    number = order + 1
    matrix = np.zeros((number, number))
    for row_index in range(number):
        for col_index in range(number):
            if row_index != col_index:
                matrix[row_index, col_index] = values[row_index] / (
                    values[col_index] * (points[row_index] - points[col_index])
                )
    matrix[0, 0] = -order * (order + 1) / 4.0
    matrix[order, order] = order * (order + 1) / 4.0
    return matrix


def halves(array):
    array = np.asarray(array, np.float32)
    high = array.astype(ml_dtypes.bfloat16)
    low = (array - high.astype(np.float32)).astype(ml_dtypes.bfloat16)
    return high, low


@functools.lru_cache(maxsize=None)
def constants():
    wave = np.arange(MODES)
    freq = (wave + 1) // 2
    phase = freq[:, None] * np.arange(PLANES)[None, :] % PLANES
    angle = 2.0 * np.pi / PLANES * phase
    table = np.where((wave % 2 == 0)[:, None], np.cos(angle), np.sin(angle))
    table = table * np.where(wave == 0, math.sqrt(1.0 / PLANES), math.sqrt(2.0 / PLANES))[:, None]
    high, low = halves(table)
    there = np.stack([high, low]).reshape(2, MODES, PLANES // CHUNK, CHUNK).transpose(0, 2, 1, 3)
    back = np.stack([high.T, low.T]).reshape(2, PLANES, MODES // CHUNK, CHUNK).transpose(0, 2, 1, 3)
    dmat = gll_matrix(ORDER).astype(np.float32)
    eye = np.eye(NP, dtype=np.float32)
    grad = np.zeros((2, ROWS, ROWS), np.float32)
    grad[0, :NODES, :NODES] = np.kron(dmat, eye)
    grad[1, :NODES, :NODES] = np.kron(eye, dmat)
    ghigh, glow = halves(grad.reshape(2 * ROWS, ROWS))
    gmat = np.zeros((4 * ROWS, 2 * KROWS), ml_dtypes.bfloat16)
    gmat[: 2 * ROWS, :ROWS] = ghigh
    gmat[: 2 * ROWS, KROWS : KROWS + ROWS] = ghigh
    gmat[2 * ROWS :, :ROWS] = glow
    dhigh, dlow = halves(grad.transpose(2, 0, 1).reshape(ROWS, 2 * ROWS))
    dmat2 = np.zeros((2 * KROWS, 2 * ROWS), ml_dtypes.bfloat16)
    dmat2[:ROWS] = dhigh
    dmat2[KROWS : KROWS + ROWS] = dlow
    return np.ascontiguousarray(there), np.ascontiguousarray(back), gmat, dmat2


def split(value):
    high = value.astype(BF16)
    return high, (value - high.astype(F32)).astype(BF16)


def split_rows(value):
    high = value.astype(BF16).astype(F32)
    gap = jnp.zeros((KROWS - ROWS, value.shape[1]), F32)
    return jnp.concatenate([high, gap, value - high, gap], axis=0).astype(BF16)


def mm(a, b):
    return jnp.dot(a, b, preferred_element_type=F32)


def fold(value):
    total = jnp.sum(value.reshape(ROWS // 8, 8, value.shape[1]), axis=0)
    out = total[:, :LANES]
    for at in range(1, value.shape[1] // LANES):
        out = out + total[:, at * LANES : (at + 1) * LANES]
    return out


def position(rank, second):
    row, side = rank // 2, rank % 2
    return row * AZ + (1 + side if second else (AZ - 1) * side)


def kernel(
    size_e,
    velx_hbm,
    vely_hbm,
    met_hbm,
    slots,
    there_hbm,
    back_hbm,
    gmat_hbm,
    dmat_hbm,
    b_x,
    b_y,
    y_x,
    y_y,
    coef,
    vel,
    met,
    there,
    back,
    gmat,
    dmat,
    snd,
    rv,
    act,
    wave,
    pgeo,
    geo,
    wts,
    ret,
    rv2,
    pack,
    bf,
    yf,
    hs,
    hr,
    acc,
    part,
    gat,
    in_sem,
    s1,
    r1,
    own,
    s2,
    r2,
    hsem,
    hrem,
    as_all,
    ar_all,
    known,
    inverse,
    esnd,
    ercv,
    es,
    er,
):
    outs_b, outs_y = (b_x, b_y), (y_x, y_y)
    me_e = lax.axis_index("elem")
    me = lax.axis_index("mode")
    chip, core = me // 2, me % 2
    zed, why = me_e % ZRING, me_e // ZRING
    size_y = size_e // ZRING
    left = (me_e + size_e - 1) % size_e
    right = (me_e + 1) % size_e
    peers = [
        (((chip + dc) % 4) * 2 + (core + cc) % 2)
        for dc, cc in ((2, 0), (2, 1), (1, 0), (3, 0), (1, 1), (3, 1), (0, 1))
    ]
    z_peers = [why * ZRING + (zed + k) % ZRING for k in (4, 3, 5, 2, 6, 1, 7)]
    y_peers = [((why + k) % size_y) * ZRING + zed for k in range(1, size_y)]

    def hops(step):
        return min(step[0], size_y - step[0]) + min(step[1], ZRING - step[1])

    steps = [(dy, dz) for dy in range(size_y) for dz in range(ZRING) if dy or dz]
    all_peers = [
        ((why + dy) % size_y) * ZRING + (zed + dz) % ZRING
        for dy, dz in sorted(steps, key=lambda step: -hops(step))
    ]

    loads = [
        pltpu.make_async_copy(velx_hbm, vel.at[0], in_sem.at[0]),
        pltpu.make_async_copy(vely_hbm, vel.at[1], in_sem.at[1]),
        pltpu.make_async_copy(met_hbm, met, in_sem.at[2]),
        pltpu.make_async_copy(gmat_hbm, gmat, in_sem.at[3]),
        pltpu.make_async_copy(dmat_hbm, dmat, in_sem.at[4]),
        pltpu.make_async_copy(there_hbm, there, in_sem.at[5]),
        pltpu.make_async_copy(back_hbm, back, in_sem.at[6]),
    ]
    for copy in loads[:5]:
        copy.start()

    tail = jnp.zeros((2, 8, LANES), F32)
    for p in range(ELEMS):
        snd[p, :, ROWS - 8 :, :] = tail
        rv[p // 2, p % 2, :, ROWS - 8 :, :] = tail

    barrier = pltpu.get_barrier_semaphore()
    for peer in peers:
        pl.semaphore_signal(barrier, inc=1, device_id=(me_e, peer), device_id_type=MESH)
    for peer in z_peers + y_peers + [left, right]:
        pl.semaphore_signal(barrier, inc=1, device_id=(peer, me), device_id_type=MESH)

    pl.semaphore_wait(barrier, len(peers) + len(z_peers) + len(y_peers) + 2)

    for peer in y_peers:
        pl.semaphore_signal(known, inc=1, device_id=(peer, me), device_id_type=MESH)

    loads[0].wait()
    loads[1].wait()

    def gather(p):
        slot = slots[p]
        for c in range(2):
            snd[p, c, 0:NODES, :] = vel[c, pl.ds(slot, NODES, stride=ELEMS), :]

    sends = []
    arrivals = [[], []]
    locals_ = []
    for e in range(2):
        for k, peer in enumerate(peers):
            p = position(peer, e)
            gather(p)
            copy = pltpu.make_async_remote_copy(
                src_ref=snd.at[p, :, pl.ds(0, NODES)],
                dst_ref=rv.at[me, e, :, pl.ds(0, NODES)],
                send_sem=s1.at[e, k],
                recv_sem=r1.at[e, me],
                device_id=(me_e, peer),
                device_id_type=MESH,
            )
            copy.start()
            sends.append(copy)
        p = position(me, e)
        gather(p)
        copy = pltpu.make_async_copy(
            snd.at[p, :, pl.ds(0, NODES)], rv.at[me, e, :, pl.ds(0, NODES)], own.at[e]
        )
        copy.start()
        locals_.append(copy)
        for k, peer in enumerate(peers):
            arrivals[e].append(
                pltpu.make_async_remote_copy(
                    src_ref=snd.at[0, :, pl.ds(0, NODES)],
                    dst_ref=rv.at[peer, e, :, pl.ds(0, NODES)],
                    send_sem=s1.at[e, k],
                    recv_sem=r1.at[e, peer],
                    device_id=(me_e, peer),
                    device_id_type=MESH,
                )
            )

    loads[5].start()
    loads[6].start()

    loads[2].wait()
    loads[3].wait()
    loads[4].wait()
    row16 = lax.broadcasted_iota(jnp.int32, (ELEMS, LANES), 0)

    def picker(p):
        return jnp.where(row16 == slots[p], 1.0, 0.0).astype(BF16)

    def spread(factors, pick):
        gap = jnp.zeros((ELEMS, ROWS - NODES), F32)
        full = jnp.concatenate([factors, gap], axis=1).T
        high = full.astype(BF16)
        rest = full - high.astype(F32)
        mid = rest.astype(BF16)
        low = (rest - mid.astype(F32)).astype(BF16)
        return mm(high, pick) + mm(mid, pick) + mm(low, pick)

    mine = jnp.concatenate([picker(position(me, 0)), picker(position(me, 1))], axis=1)
    jac = spread(met[7], mine)
    for g in range(4):
        full = spread(met[g], mine) * jac
        pgeo[0, g] = full[:, :LANES]
        pgeo[1, g] = full[:, LANES:]

    def spread_row(r, carry):
        pick = jnp.concatenate([picker(r * AZ + a) for a in range(AZ)], axis=1)
        for g in range(4):
            full = spread(met[4 + g], pick)
            for a in range(AZ):
                geo[g, r * AZ + a] = full[:, a * LANES : (a + 1) * LANES]
        return carry

    lax.fori_loop(0, RAD, spread_row, 0)

    node = lax.broadcasted_iota(jnp.int32, (ROWS, LANES), 0)
    along = node % NP
    sides = jnp.where((along == 0) | (along == NP - 1), 0.5, 1.0).astype(F32)
    sides = jnp.where(node < NODES, sides, 0.0)
    first, last = node < NP, node >= EDGE
    wts[0] = jnp.where(first, 0.0, jnp.where(last, 0.5, 1.0)) * sides
    wts[1] = jnp.where(first | last, 0.5, 1.0) * sides
    wts[2] = wts[1]
    wts[3] = jnp.where(last, 0.0, jnp.where(first, 0.5, 1.0)) * sides

    lane = lax.broadcasted_iota(jnp.int32, (1, LANES), 1) + me * LANES
    freq = ((lane + 1) // 2).astype(F32) / WAVE
    lam = SIGMA + freq * freq

    acc[...] = jnp.zeros_like(acc)

    stored = [slots[p] for p in range(ELEMS)]
    for s in range(ELEMS):
        place = jnp.int32(0)
        for p in range(1, ELEMS):
            place = jnp.where(stored[p] == s, jnp.int32(p), place)
        inverse[s] = place

    def prior(p, carry):
        twice = SIGMA * geo[3, p]
        for c in range(2):
            bf[c, p] = twice * snd[p, c]
        return carry

    lax.fori_loop(0, ELEMS, prior, 0)

    ret_sends = []
    ret_locals = [[], []]

    side = me % 2

    def send_back(e, c):
        start = 1 - side if e else side

        def pack_rank(rank, carry):
            for i in range(NP):
                pack[e, rank, c, 8 * i : 8 * i + 8] = ret[e, rank, c, pl.ds(NP * i + start, 8), :]
            return carry

        lax.fori_loop(0, GROUPS, pack_rank, 0, unroll=2)
        for k, peer in enumerate(peers):
            copy = pltpu.make_async_remote_copy(
                src_ref=pack.at[e, peer, c],
                dst_ref=rv2.at[position(me, e), c],
                send_sem=s2.at[e, c, k],
                recv_sem=r2.at[e, c, me],
                device_id=(me_e, peer),
                device_id_type=MESH,
            )
            copy.start()
            ret_sends.append(copy)
        copy = pltpu.make_async_copy(
            pack.at[e, me, c],
            rv2.at[position(me, e), c],
            own.at[2 + 2 * e + c],
        )
        copy.start()
        ret_locals[c].append(copy)
    for e in range(2):
        for copy in arrivals[e]:
            copy.wait_recv()
        locals_[e].wait()
        for src in range(GROUPS):
            both = rv[src, e].reshape(2 * ROWS, LANES)
            high, low = split(both)
            act[0 : 2 * ROWS, src * LANES : (src + 1) * LANES] = high
            act[2 * ROWS :, src * LANES : (src + 1) * LANES] = low
        if e == 0:
            loads[5].wait()

        def planes(z, carry, e=e):
            top = mm(act[...], there[0, z])
            field = top[: 2 * ROWS] + top[2 * ROWS :] + mm(act[0 : 2 * ROWS, :], there[1, z])
            u, v = field[:ROWS], field[ROWS:]
            diff = mm(gmat[...], split_rows(jnp.concatenate([u, v], axis=1)))
            diff = diff[: 2 * ROWS] + diff[2 * ROWS :]
            m = [jnp.concatenate([pgeo[e, g]] * (CHUNK // LANES), axis=1) for g in range(4)]
            by_i = u * m[0] + v * m[2]
            by_j = u * m[1] + v * m[3]
            for c in range(2):
                cols = slice(c * CHUNK, (c + 1) * CHUNK)
                prod = by_i * diff[:ROWS, cols] + by_j * diff[ROWS:, cols]
                at = pl.ds(pl.multiple_of(z * CHUNK, CHUNK), CHUNK)
                wave[c * 2 * KROWS : (c + 1) * 2 * KROWS, at] = split_rows(prod)
            return carry

        lax.fori_loop(0, PLANES // CHUNK, planes, 0, unroll=3)
        if e == 0:
            loads[6].wait()

        for c in range(2):
            for step, dc in enumerate((2, 1, 3, 0)):
                n = (chip + dc) % 4
                top = mm(wave[c * 2 * KROWS : (c + 1) * 2 * KROWS, :], back[0, n])
                low = mm(wave[c * 2 * KROWS : c * 2 * KROWS + KROWS, :], back[1, n])
                hat = top[:ROWS] + top[KROWS : KROWS + ROWS] + low[:ROWS]
                for half in range(2):
                    ret[e, n * 2 + half, c] = hat[:, half * LANES : (half + 1) * LANES]
            if e == 0:
                send_back(e, c)
        if e == 1:
            near = pl.ds(side * (NP - 1), NP, stride=NP)
            far = pl.ds((1 - side) * (NP - 1), NP, stride=NP)
            for rank in range(GROUPS):
                for c in range(2):
                    esnd[rank, c, 0:NP] = ret[1, rank, c, near, :] + ret[0, rank, c, far, :]
            for k, peer in enumerate(peers):
                copy = pltpu.make_async_remote_copy(
                    src_ref=esnd.at[peer, :, pl.ds(0, NP)],
                    dst_ref=ercv.at[me, :, pl.ds(0, NP)],
                    send_sem=es.at[k],
                    recv_sem=er.at[me],
                    device_id=(me_e, peer),
                    device_id_type=MESH,
                )
                copy.start()
                ret_sends.append(copy)
            for c in range(2):
                ercv[me, c, 0:NP] = esnd[me, c, 0:NP]
                send_back(e, c)

    def wait_returns(e, c):
        for peer in peers:
            pltpu.make_async_remote_copy(
                src_ref=pack.at[e, 0, c],
                dst_ref=rv2.at[position(peer, e), c],
                send_sem=s2.at[e, c, 0],
                recv_sem=r2.at[e, c, peer],
                device_id=(me_e, peer),
                device_id_type=MESH,
            ).wait_recv()
        ret_locals[c][e].wait()

    halo_sends = []

    def radial(field, c, cols):
        for a in cols:
            for r in range(RAD - 1):
                up, down = r * AZ + a, (r + 1) * AZ + a
                joined = field[c, up, EDGE : EDGE + 8] + field[c, down, 0:8]
                corner = field[c, up, EDGE + 8 : NODES] + field[c, down, 8:NP]
                field[c, up, EDGE : EDGE + 8] = joined
                field[c, down, 0:8] = joined
                field[c, up, EDGE + 8 : NODES] = corner
                field[c, down, 8:NP] = corner
            field[c, a, 0:8] = jnp.zeros((8, LANES), F32)
            field[c, a, 8:NP] = jnp.zeros((1, LANES), F32)
            end = (RAD - 1) * AZ + a
            field[c, end, EDGE : EDGE + 8] = jnp.zeros((8, LANES), F32)
            field[c, end, EDGE + 8 : NODES] = jnp.zeros((1, LANES), F32)

    first_edge = pl.ds(0, NP, stride=NP)
    last_edge = pl.ds(NP - 1, NP, stride=NP)

    def rims_start(field, c, which):
        for r in range(RAD):
            hs[which, c, 0, r, 0:NP] = field[c, r * AZ, first_edge, :]
            hs[which, c, 1, r, 0:NP] = field[c, r * AZ + AZ - 1, last_edge, :]
        copies = []
        for side, peer in ((0, left), (1, right)):
            copy = pltpu.make_async_remote_copy(
                src_ref=hs.at[which, c, side, :, pl.ds(0, NP)],
                dst_ref=hr.at[which, c, side, :, pl.ds(0, NP)],
                send_sem=hsem.at[which, c, side],
                recv_sem=hrem.at[which, c, side],
                device_id=(peer, me),
                device_id_type=MESH,
            )
            copy.start()
            copies.append(copy)
        halo_sends.extend(copies)
        return copies

    def joints(field, c):
        for r in range(RAD):
            for a in range(AZ - 1):
                p = r * AZ + a
                shared = field[c, p, last_edge, :] + field[c, p + 1, first_edge, :]
                field[c, p, last_edge, :] = shared
                field[c, p + 1, first_edge, :] = shared

    def rims_finish(field, c, which, copies):
        for copy in copies:
            copy.wait_recv()
        for r in range(RAD):
            p = r * AZ + AZ - 1
            field[c, p, last_edge, :] = field[c, p, last_edge, :] + hr[which, c, 0, r, 0:NP]
            p = r * AZ
            field[c, p, first_edge, :] = field[c, p, first_edge, :] + hr[which, c, 1, r, 0:NP]

    def pair(ref, c, p0, p1):
        return jnp.concatenate([ref[c, p0], ref[c, p1]], axis=1)

    def fluxes(x, p0, p1):
        diff = mm(gmat[...], split_rows(x))
        diff = diff[: 2 * ROWS] + diff[2 * ROWS :]
        x_i, x_j = diff[:ROWS], diff[ROWS:]
        g = [pair(geo, k, p0, p1) for k in range(4)]
        return x_i, x_j, g[0] * x_i + g[1] * x_j, g[1] * x_i + g[2] * x_j, g[3]

    lam2 = jnp.concatenate([lam, lam], axis=1)

    def weights(r):
        return jnp.concatenate([wts[r], wts[r]], axis=1)

    def apply(c, cols):
        def step(r, carry):
            p0, p1 = r * AZ + cols[0], r * AZ + cols[1]
            x = pair(bf, c, p0, p1)
            x_i, x_j, f_i, f_j, jw = fluxes(x, p0, p1)
            high, low = split(jnp.concatenate([f_i, f_j], axis=0))
            top = mm(dmat[...], high)
            y = top[:ROWS] + top[KROWS : KROWS + ROWS] + mm(dmat[0:KROWS, :], low)[:ROWS]
            y = y + lam2 * jw * x
            yf[c, p0] = y[:, :LANES]
            yf[c, p1] = y[:, LANES:]
            acc[c, 0] = acc[c, 0] + fold(x * x * weights(r))
            acc[c, 1] = acc[c, 1] + fold(x * y)
            return carry

        lax.fori_loop(0, RAD, step, 0, unroll=4)

    def energy(c, cols):
        def step(r, carry):
            p0, p1 = r * AZ + cols[0], r * AZ + cols[1]
            y = pair(yf, c, p0, p1)
            y_i, y_j, f_i, f_j, jw = fluxes(y, p0, p1)
            acc[c, 2] = acc[c, 2] + fold(y * y * weights(r))
            acc[c, 3] = acc[c, 3] + fold(f_i * y_i + f_j * y_j + lam2 * jw * y * y)
            return carry

        lax.fori_loop(0, RAD, step, 0, unroll=4)

    def rhs(c, cols):
        for r in range(RAD):
            for a in cols:
                p = r * AZ + a
                for i in range(NP):
                    at = slice(NP * i + a % 2, NP * i + a % 2 + 8)
                    bf[c, p, at] = bf[c, p, at] - rv2[p, c, 8 * i : 8 * i + 8]
        radial(bf, c, cols)

    inside, outside = (1, 2), (0, AZ - 1)
    b_flights, y_flights = [], []
    for c in range(2):
        wait_returns(0, c)
        rhs(c, outside)
        b_flights.append(rims_start(bf, c, 0))
    for peer in peers:
        pltpu.make_async_remote_copy(
            src_ref=esnd.at[peer, :, pl.ds(0, NP)],
            dst_ref=ercv.at[peer, :, pl.ds(0, NP)],
            send_sem=es.at[0],
            recv_sem=er.at[peer],
            device_id=(me_e, peer),
            device_id_type=MESH,
        ).wait_recv()

    seams = ((0, last_edge, 1, first_edge), (AZ - 1, first_edge, AZ - 2, last_edge))

    def outer_seams(c):
        for side, (outer, edge_o, inner, edge_i) in enumerate(seams):
            terms = [
                bf[c, r * AZ + inner, edge_i, :] - ercv[2 * r + side, c, 0:NP] for r in range(RAD)
            ]
            zero = jnp.zeros((1, LANES), F32)
            joins = [zero] + [terms[r][NP - 1 :] + terms[r + 1][:1] for r in range(RAD - 1)] + [zero]
            for r in range(RAD):
                whole = jnp.concatenate([joins[r], terms[r][1 : NP - 1], joins[r + 1]], axis=0)
                p = r * AZ + outer
                bf[c, p, edge_o, :] = bf[c, p, edge_o, :] + whole

    def inner_joints(c):
        for r in range(RAD):
            for outer, edge_o, inner, edge_i in seams:
                bf[c, r * AZ + inner, edge_i, :] = bf[c, r * AZ + outer, edge_o, :]
            p = r * AZ + 1
            shared = bf[c, p, last_edge, :] + bf[c, p + 1, first_edge, :]
            bf[c, p, last_edge, :] = shared
            bf[c, p + 1, first_edge, :] = shared

    for c in range(2):
        outer_seams(c)
    for c in range(2):
        rims_finish(bf, c, 0, b_flights[c])
        apply(c, outside)
        radial(yf, c, outside)
        y_flights.append(rims_start(yf, c, 1))
    for c in range(2):
        wait_returns(1, c)
        rhs(c, inside)
        inner_joints(c)
        apply(c, inside)
        radial(yf, c, inside)
        joints(yf, c)
        energy(c, inside)
    rims_finish(yf, 0, 1, y_flights[0])
    rims_finish(yf, 1, 1, y_flights[1])
    energy(0, outside)
    energy(1, outside)

    sums = jnp.concatenate(
        [jnp.sum(acc[c, k], axis=0, keepdims=True) for c in range(2) for k in range(4)], axis=0
    )

    part[...] = sums
    if y_peers:
        pl.semaphore_wait(known, len(y_peers))
    for k, peer in enumerate(all_peers):
        copy = pltpu.make_async_remote_copy(
            src_ref=part,
            dst_ref=gat.at[me_e],
            send_sem=as_all.at[k],
            recv_sem=ar_all.at[me_e],
            device_id=(peer, me),
            device_id_type=MESH,
        )
        copy.start()
        halo_sends.append(copy)
    gat[me_e] = sums
    for c in range(2):

        def store(s, carry, c=c):
            p = inverse[s]
            at = pl.ds(s, NODES, stride=ELEMS)
            outs_b[c][at, :] = bf[c, p, 0:NODES]
            outs_y[c][at, :] = yf[c, p, 0:NODES]
            return carry

        lax.fori_loop(0, ELEMS, store, 0, unroll=4)
    for k, peer in enumerate(all_peers):
        pltpu.make_async_remote_copy(
            src_ref=part,
            dst_ref=gat.at[peer],
            send_sem=as_all.at[k],
            recv_sem=ar_all.at[peer],
            device_id=(peer, me),
            device_id_type=MESH,
        ).wait_recv()
    sums = jnp.sum(gat[...], axis=0)

    for c in range(2):
        m0, m1, m2, m3 = (sums[c * 4 + k : c * 4 + k + 1] for k in range(4))
        alpha = m0 / m1
        grown = alpha * alpha * m2 - m0
        scale = 1.0 + grown / m0
        below = scale * scale * m1 - 2.0 * scale * alpha * m2 + alpha * alpha * m3
        beyond = grown / below
        on_b = alpha + beyond * scale
        on_y = -beyond * alpha

        coef[2 * c : 2 * c + 1] = on_b
        coef[2 * c + 1 : 2 * c + 2] = on_y

    for copy in sends + ret_sends + halo_sends:
        copy.wait_send()


def combine_kernel(b_x, b_y, y_x, y_y, coef, out_x, out_y, held, sem):
    size = b_x.shape[0] // PIECES
    copies = []
    for piece in range(PIECES):
        at = pl.ds(piece * size, size)
        for c, (b, y, out) in enumerate(((b_x, y_x, out_x), (b_y, y_y, out_y))):
            held[c, at] = coef[2 * c : 2 * c + 1] * b[at] + coef[2 * c + 1 : 2 * c + 2] * y[at]
            copy = pltpu.make_async_copy(held.at[c, at], out.at[at], sem.at[c, piece])
            copy.start()
            copies.append(copy)
    for copy in copies:
        copy.wait()


def body(size_e, vel_x, vel_y, metrics, slot_order):
    there, back, gmat, dmat = constants()
    any_space = pl.BlockSpec(memory_space=pl.ANY)
    vmem = pl.BlockSpec(memory_space=pltpu.VMEM)
    smem = pl.BlockSpec(memory_space=pltpu.SMEM)
    dma = pltpu.SemaphoreType.DMA
    rows = NODES * ELEMS
    b_x, b_y, y_x, y_y, coef = pl.pallas_call(
        functools.partial(kernel, size_e),
        out_shape=[pltpu.VMEM((rows, LANES), F32)] * 4 + [pltpu.VMEM((8, LANES), F32)],
        in_specs=[any_space] * 3 + [smem] + [any_space] * 4,
        out_specs=[vmem] * 5,
        scratch_shapes=[
            pltpu.VMEM((2, rows, LANES), F32),
            pltpu.VMEM((8, ELEMS, NODES), F32),
            pltpu.VMEM(there.shape, BF16),
            pltpu.VMEM(back.shape, BF16),
            pltpu.VMEM(gmat.shape, BF16),
            pltpu.VMEM(dmat.shape, BF16),
            pltpu.VMEM((ELEMS, 2, ROWS, LANES), F32),
            pltpu.VMEM((GROUPS, 2, 2, ROWS, LANES), F32),
            pltpu.VMEM((4 * ROWS, MODES), BF16),
            pltpu.VMEM((4 * KROWS, PLANES), BF16),
            pltpu.VMEM((2, 4, ROWS, LANES), F32),
            pltpu.VMEM((4, ELEMS, ROWS, LANES), F32),
            pltpu.VMEM((RAD, ROWS, LANES), F32),
            pltpu.VMEM((2, GROUPS, 2, ROWS, LANES), F32),
            pltpu.VMEM((ELEMS, 2, NP * ORDER, LANES), F32),
            pltpu.VMEM((2, GROUPS, 2, NP * ORDER, LANES), F32),
            pltpu.VMEM((2, ELEMS, ROWS, LANES), F32),
            pltpu.VMEM((2, ELEMS, ROWS, LANES), F32),
            pltpu.VMEM((2, 2, 2, RAD, 16, LANES), F32),
            pltpu.VMEM((2, 2, 2, RAD, 16, LANES), F32),
            pltpu.VMEM((2, 4, 8, LANES), F32),
            pltpu.VMEM((8, LANES), F32),
            pltpu.VMEM((size_e, 8, LANES), F32),
            dma((7,)),
            dma((2, GROUPS)),
            dma((2, GROUPS)),
            dma((6,)),
            dma((2, 2, GROUPS)),
            dma((2, 2, GROUPS)),
            dma((2, 2, 2)),
            dma((2, 2, 2)),
            dma((size_e,)),
            dma((size_e,)),
            pltpu.SemaphoreType.REGULAR,
            pltpu.SMEM((ELEMS,), jnp.int32),
            pltpu.VMEM((GROUPS, 2, 16, LANES), F32),
            pltpu.VMEM((GROUPS, 2, 16, LANES), F32),
            dma((GROUPS,)),
            dma((GROUPS,)),
        ],
        compiler_params=pltpu.CompilerParams(
            collective_id=0, has_side_effects=True, vmem_limit_bytes=56 * 2**20
        ),
    )(
        vel_x.reshape(rows, LANES),
        vel_y.reshape(rows, LANES),
        metrics.transpose(0, 2, 1),
        slot_order,
        jnp.asarray(there),
        jnp.asarray(back),
        jnp.asarray(gmat),
        jnp.asarray(dmat),
    )
    out_x, out_y = pl.pallas_call(
        combine_kernel,
        out_shape=[jax.ShapeDtypeStruct((rows, LANES), F32)] * 2,
        in_specs=[vmem] * 5,
        out_specs=[any_space] * 2,
        scratch_shapes=[pltpu.VMEM((2, rows, LANES), F32), dma((2, PIECES))],
        compiler_params=pltpu.CompilerParams(vmem_limit_bytes=16 * 2**20),
    )(b_x, b_y, y_x, y_y, coef)
    shape = (NODES, ELEMS, LANES)
    return out_x.reshape(shape), out_y.reshape(shape)


def solution(mesh):
    placed = (P(None, "elem", "mode"), P(None, "elem", "mode"), P(None, None, "elem"), P("elem"))
    return jax.shard_map(
        functools.partial(body, mesh.shape["elem"]),
        mesh=mesh,
        in_specs=placed,
        out_specs=(P(None, "elem", "mode"), P(None, "elem", "mode")),
        check_vma=False,
    )
```
